512 devices in a mesh: dp: 4 (over x), fsdp: 128 (over z, y, core).
Axes of the slice: x: 4, y: 8, z: 8, core: 2. Of those that a mesh axis runs over, the one named last changes fastest.
Arguments:
- gradient: bfloat16 [4, 8, 512, 8192], P('dp', None, 'fsdp'), may hold values from -6 to 6
- owner_slot: int32 [8, 16], replicated, may hold values from 0 to 255, as said below
- stat_left: float32 [256, 512, 512], P('fsdp', 'dp'), may hold values from -12 to 12
- stat_right: float32 [256, 512, 512], P('fsdp', 'dp'), may hold values from -12 to 12
- second_moment: float32 [256, 512, 512], P('fsdp', 'dp'), may hold values from 0.05 to 1
- basis_left: bfloat16 [256, 512, 512], P('fsdp', None, 'dp'), may hold values from -0.25 to 0.25
- basis_right: bfloat16 [256, 512, 512], P('fsdp', 'dp'), may hold values from -0.25 to 0.25
Outputs:
- update: bfloat16 [8, 512, 16, 512], P(None, 'fsdp', None, 'dp')
- new_left: float32 [256, 512, 512], P('fsdp', 'dp')
- new_right: float32 [256, 512, 512], P('fsdp', 'dp')
- new_moment: float32 [256, 512, 512], P('fsdp', 'dp')
The draws below stay inside these ranges and needn't reach their ends.
Inputs may be any that keep to these rules, and one draw needn't show every extreme that they name: `owner_slot`: 128 distinct slot numbers; slot s belongs to fsdp index s // 2. A quarter of the fsdp indices, always including the first and the last, own 2 blocks, half own 1, a quarter own none; which slots of an index are used is drawn from the seed.
All inputs are finite; a program needn't handle non-finite values.
Results may differ from the reference program's by a relative error of at most 0.022.
Values may be sent and summed in bfloat16 or wider, within the bound.
A program may use at most 64 MiB of HBM per device.

```python
import math
import jax
import jax.numpy as jnp
from jax import lax

D = 8192
BLOCK = 512
COL_BLOCKS = 16
LAYERS = 8
BLOCKS = 128
SLOTS_DEV = 2
N_DP = 4
N_FSDP = 128


def draw_owner_slot(key, part):
    key = jax.random.fold_in(key, 7)
    key_order, key_local, key_blocks = jax.random.split(key, 3)
    owners = 2 * BLOCKS // SLOTS_DEV
    middle_order = (jax.random.permutation(key_order, owners - 2) + 1).astype(jnp.int32)
    ranking = jnp.concatenate([jnp.array([0, owners - 1], jnp.int32), middle_order])
    position = jnp.zeros((owners,), jnp.int32).at[ranking].set(jnp.arange(owners, dtype=jnp.int32))
    counts = jnp.where(position < owners // 4, SLOTS_DEV, jnp.where(position < 3 * owners // 4, SLOTS_DEV // 2, 0))
    scores = jax.random.randint(key_local, (owners, SLOTS_DEV), 0, 1 << 20) * SLOTS_DEV
    scores = scores + jnp.arange(SLOTS_DEV, dtype=jnp.int32)[None, :]
    local_rank = jnp.argsort(jnp.argsort(scores, axis=1), axis=1)
    chosen = (local_rank < counts[:, None]).reshape(-1)
    picked = jnp.nonzero(chosen, size=BLOCKS)[0].astype(jnp.int32)
    mixing = jax.random.permutation(key_blocks, BLOCKS)
    return picked[mixing].reshape(LAYERS, COL_BLOCKS).astype(jnp.int32)


def steps_of(stream_key, shape, pieces, smallest, top_value):
    loudness, own = 1.0, jax.random.fold_in(stream_key, 6)
    for dim, shards_of in pieces:
        draws = jnp.exp(jax.random.uniform(jax.random.fold_in(own, dim), (shards_of,), jnp.float32, smallest / len(pieces), top_value / len(pieces)))
        loudness = loudness * jnp.repeat(draws, shape[dim] // shards_of).reshape([-1 if axis == dim else 1 for axis in range(len(shape))])
    return loudness


def scatter_about(key, extent, deviation, limit, cuts=(), held_as=jnp.bfloat16):
    entries = jax.random.normal(key, extent, jnp.float32) * deviation
    if len(cuts) > 0:
        entries = steps_of(key, extent, cuts, -0.22, 0.18) * entries
    return jnp.clip(entries, min=-limit, max=limit).astype(held_as)


def setup_inputs(seed: int = 0) -> dict:
    splits = jax.random.split(jax.random.key(seed), 8)
    gradient = scatter_about(splits[0], (N_DP, LAYERS, BLOCK, D), 1.0, 6.0, ((0, 4), (2, 128)))
    owner_slot = draw_owner_slot(jax.random.fold_in(splits[7], 71), 0)
    stat_left = scatter_about(splits[2], (SLOTS_DEV * N_FSDP, BLOCK, BLOCK), 2.0, 12.0, ((0, 128), (1, 4)), jnp.float32)
    stat_right = scatter_about(splits[3], (SLOTS_DEV * N_FSDP, BLOCK, BLOCK), 2.0, 12.0, ((0, 128), (1, 4)), jnp.float32)
    second_moment = jnp.clip(jnp.exp(math.log(1.0) - 2.9957323 * jax.random.uniform(splits[4], (SLOTS_DEV * N_FSDP, BLOCK, BLOCK), jnp.float32) ** steps_of(splits[4], (SLOTS_DEV * N_FSDP, BLOCK, BLOCK), ((0, 128), (1, 4)), -0.2, 0.2)), 0.05, 1.0)
    basis_left = scatter_about(splits[5], (SLOTS_DEV * N_FSDP, BLOCK, BLOCK), BLOCK ** -0.5, 0.25, ((0, 128), (2, 4)))
    basis_right = scatter_about(splits[6], (SLOTS_DEV * N_FSDP, BLOCK, BLOCK), BLOCK ** -0.5, 0.25, ((0, 128), (1, 4)))
    return {"gradient": gradient, "owner_slot": owner_slot, "stat_left": stat_left, "stat_right": stat_right, "second_moment": second_moment, "basis_left": basis_left, "basis_right": basis_right}


def per_block(items):
    block, left, right, moment, qleft, qright = items
    wide = block.astype(jnp.float32)
    qleft_wide = qleft.astype(jnp.float32)
    qright_wide = qright.astype(jnp.float32)
    left_next = 0.95 * left + 0.05 * jnp.dot(wide, wide.T, preferred_element_type=jnp.float32)
    right_next = 0.95 * right + 0.05 * jnp.dot(wide.T, wide, preferred_element_type=jnp.float32)
    half_turn = jnp.dot(qleft_wide.T, wide, preferred_element_type=jnp.float32).astype(jnp.bfloat16)
    rotated = jnp.dot(half_turn.astype(jnp.float32), qright_wide, preferred_element_type=jnp.float32)
    moment_next = 0.95 * moment + 0.05 * rotated * rotated
    scaled = (rotated / (jnp.sqrt(moment_next) + 1e-08)).astype(jnp.bfloat16)
    back_turn = jnp.dot(scaled.astype(jnp.float32), qright_wide.T, preferred_element_type=jnp.float32).astype(jnp.bfloat16)
    result = jnp.dot(qleft_wide, back_turn.astype(jnp.float32), preferred_element_type=jnp.float32).astype(jnp.bfloat16)
    return (left_next, right_next, moment_next, result)

def reference(gradient, owner_slot, stat_left, stat_right, second_moment, basis_left, basis_right):
    summed = lax.optimization_barrier(jnp.sum(gradient.astype(jnp.float32), axis=0)) / N_DP
    blocks = summed.astype(jnp.bfloat16).reshape(LAYERS, BLOCK, COL_BLOCKS, BLOCK)
    blocks = jnp.transpose(blocks, (0, 2, 1, 3)).reshape(BLOCKS, BLOCK, BLOCK)
    slot_flat = owner_slot.reshape(-1).astype(jnp.int32)
    left_next, right_next, moment_next, result = lax.map(per_block, (blocks, stat_left[slot_flat], stat_right[slot_flat], second_moment[slot_flat], basis_left[slot_flat], basis_right[slot_flat]))
    new_left = stat_left.at[slot_flat].set(left_next)
    new_right = stat_right.at[slot_flat].set(right_next)
    new_moment = second_moment.at[slot_flat].set(moment_next)
    update = jnp.transpose(result.reshape(LAYERS, COL_BLOCKS, BLOCK, BLOCK), (0, 2, 1, 3))
    return (update, new_left, new_right, new_moment)
```

```python
import functools

import jax
import jax.numpy as jnp
from jax import lax
from jax.experimental import pallas as pl
from jax.experimental.pallas import tpu as pltpu
from jax.sharding import PartitionSpec as P

epsilon = 1e-08
MESH = pl.DeviceIdType.MESH
F32, BF16, I32 = jnp.float32, jnp.bfloat16, jnp.int32
LINE = 8
LANES = 128


def iota(shape, dim):
    return lax.broadcasted_iota(I32, shape, dim)


def dot(a, b, ca=1, cb=0):
    return lax.dot_general(a, b, (((ca,), (cb,)), ((), ())), preferred_element_type=F32)


def one_hot(rows, columns):
    return jnp.where(rows == columns, 1.0, 0.0).astype(BF16)


def kernel(
    slot_ref, grad_ref, left_ref, right_ref, moment_ref, bl_ref, br_ref,
    update_ref, new_left_ref, new_right_ref, new_moment_ref,
    raw, mean, pick, place, sort_in, sort_out,
    send_b, recv_b, g_full, l_full, r_full, l_own, back_own, back_full,
    out_own, out_send, out_recv, send_e, recv_e, stat_l, stat_r, stat_m,
    local_sem, a_send, a_recv, x_send, x_recv, b_send, b_recv, c_send, c_recv,
    l_send, l_recv, r_send, r_recv, d_send, d_recv, y_send, y_recv, e_send, e_recv, ready,
):
    x = lax.axis_index("dp")
    f = lax.axis_index("fsdp")
    groups = 4
    core = lax.rem(f, 2)
    chip = f // 2
    z, y = chip // LINE, lax.rem(chip, LINE)
    chips = LINE * LINE
    sibling = (x, f + 1 - 2 * core)
    layers, rows, blocks_per, _ = grad_ref.shape
    order = g_full.shape[1]

    def x_peer(d):
        return lax.rem(x + d, groups)

    def device(zz, yy):
        return (x, (zz * LINE + yy) * 2 + core)

    def z_peer(d):
        return device(lax.rem(z + d, LINE), y)

    def y_peer(d):
        return device(z, lax.rem(y + d, LINE))

    def column(p):
        return pl.ds(pl.multiple_of(p * LANES, LANES), LANES)

    def remote(src, dst, send, recv, to):
        return pltpu.make_async_remote_copy(
            src_ref=src, dst_ref=dst, send_sem=send, recv_sem=recv,
            device_id=to, device_id_type=MESH,
        )

    def arrived(ref, sem):
        pltpu.make_async_copy(ref, ref, sem).wait()

    loads = [
        pltpu.make_async_copy(grad_ref.at[:, :, :, column(x)], raw.at[3], local_sem.at[0]),
        pltpu.make_async_copy(bl_ref, l_own, local_sem.at[1]),
        pltpu.make_async_copy(left_ref, stat_l, local_sem.at[2]),
        pltpu.make_async_copy(right_ref, stat_r, local_sem.at[3]),
        pltpu.make_async_copy(moment_ref, stat_m, local_sem.at[4]),
    ]
    for t in range(2):
        loads.append(pltpu.make_async_copy(bl_ref.at[t], l_full.at[t, :, column(x)], local_sem.at[5 + t]))
        loads.append(pltpu.make_async_copy(br_ref.at[t], r_full.at[t, column(x), :], local_sem.at[7 + t]))
    for load in loads:
        load.start()

    barrier = pltpu.get_barrier_semaphore()
    for d in range(1, groups):
        pl.semaphore_signal(barrier, inc=1, device_id=(x_peer(d), f), device_id_type=MESH)
    pl.semaphore_signal(barrier, inc=1, device_id=sibling, device_id_type=MESH)
    for d in range(1, LINE):
        pl.semaphore_signal(barrier, inc=1, device_id=z_peer(d), device_id_type=MESH)
        pl.semaphore_signal(barrier, inc=1, device_id=y_peer(d), device_id_type=MESH)
    pl.semaphore_wait(barrier, groups + 2 * (LINE - 1))

    for d in range(1, groups):
        p = x_peer(d)
        remote(grad_ref.at[:, :, :, column(p)], raw.at[d - 1], a_send, a_recv, (p, f)).start()
    for d in range(1, LINE):
        pl.semaphore_signal(ready, inc=1, device_id=y_peer(d), device_id_type=MESH)

    many = layers * rows * blocks_per
    slots = slot_ref[...].astype(F32).astype(BF16)
    spread = one_hot(lax.rem(iota((blocks_per, many), 1), blocks_per), iota((blocks_per, many), 0))
    wide = dot(slots, spread)
    own_layer = iota((layers, many), 1) // (rows * blocks_per) == iota((layers, many), 0)
    slot_lane = jnp.sum(jnp.where(own_layer, wide, 0.0), axis=0, keepdims=True).astype(I32)
    row_lane = lax.rem(iota((1, many), 1) // blocks_per, rows)
    owner_lane = slot_lane // 2
    code_lane = jnp.where(
        lax.rem(owner_lane, 2) == core,
        (owner_lane // 2) * 2 * rows + lax.rem(slot_lane, 2) * rows + row_lane, -1,
    )
    used = [jnp.max(jnp.where(slot_lane == 2 * f + t, 1.0, 0.0), axis=1, keepdims=True) for t in range(2)]
    pick[...] = one_hot(code_lane, iota((chips * 2 * rows, many), 0))
    tall_spread = one_hot(lax.rem(iota((many, blocks_per), 0), blocks_per), iota((many, blocks_per), 1))
    tall = dot(tall_spread, slots, 1, 1)
    tall_layer = iota((many, layers), 0) // (rows * blocks_per) == iota((many, layers), 1)
    slot_col = jnp.sum(jnp.where(tall_layer, tall, 0.0), axis=1, keepdims=True).astype(I32)
    row_col = lax.rem(iota((many, 1), 0) // blocks_per, rows)
    owner_col = slot_col // 2
    far = jnp.where(lax.rem(owner_col, 2) == core, 0, 1)
    code_col = ((owner_col // 2) * 2 + far) * 2 * rows + lax.rem(slot_col, 2) * rows + row_col
    place[...] = one_hot(code_col, iota((many, chips * 4 * rows), 1))
    chunk = 256
    per = chunk // (4 * rows)
    ro, co = iota((chunk, 1), 0), iota((1, chunk), 1)
    far_o = lax.rem(lax.rem(ro // rows, 2) + core, 2)
    want = ((lax.rem(ro // (2 * rows), per) * 2 + far_o) * 2 + ro // (chunk // 2)) * rows + lax.rem(ro, rows)
    sort_in[...] = one_hot(want, co)
    core_o = lax.rem(ro // (chunk // 2) + core, 2)
    chip_o = lax.rem(ro // (2 * rows), per)
    t_o = lax.rem(ro // rows, 2)
    want = ((t_o * per + chip_o) * 2 + core_o) * rows + lax.rem(ro, rows)
    sort_out[...] = one_hot(want, co)

    loads[0].wait()
    arrived(raw.at[pl.ds(0, 3)], a_recv)
    for load in loads[1:]:
        load.wait()
    total = raw[0].astype(F32) + raw[1].astype(F32) + raw[2].astype(F32) + raw[3].astype(F32)
    mean[0] = (total * (1.0 / groups)).astype(BF16).reshape(many, LANES)
    share = remote(mean.at[0], mean.at[1], x_send, x_recv, sibling)
    share.start()
    for d in range(1, groups):
        for t in range(2):
            remote(br_ref.at[t], r_full.at[t, column(x), :], r_send, r_recv, (x_peer(d), f)).start()
    for d in range(1, groups):
        for t in range(2):
            remote(bl_ref.at[t], l_full.at[t, :, column(x)], l_send, l_recv, (x_peer(d), f)).start()
    near = dot(pick[...], mean[0]).reshape(chips, 2 * rows, LANES)
    share.wait()
    away = dot(pick[...], mean[1]).reshape(chips, 2 * rows, LANES)
    send_b[...] = jnp.concatenate([near, away], axis=1).astype(BF16)

    pl.semaphore_wait(ready, LINE - 1)

    def all_to_all(src, dst, send, recv):
        def step(i, carry):
            to = lax.rem(chip + i * 37, chips)
            remote(src.at[to], dst.at[chip], send, recv, (x, to * 2 + core)).start()
            return carry
        lax.fori_loop(1, chips, step, 0)
        dst[chip] = src[chip]
        arrived(dst.at[pl.ds(0, chips - 1)], recv)

    all_to_all(send_b, recv_b, b_send, b_recv)
    for j in range(chips // per):
        part = dot(sort_in[...], recv_b[j * per : (j + 1) * per].reshape(chunk, LANES)).astype(BF16)
        half = chunk // 2
        for t in range(2):
            g_full[t, j * half : (j + 1) * half, column(x)] = part[t * half : (t + 1) * half]
    for t in range(2):
        for d in range(1, groups):
            mine = g_full.at[t, :, column(x)]
            remote(mine, mine, c_send, c_recv.at[t], (x_peer(d), f)).start()
    quarter = order // groups
    parts = pl.ds(0, order - quarter)
    for t in range(2):
        arrived(g_full.at[t, parts, :], c_recv.at[t])
        if t == 0:
            arrived(r_full.at[:, parts, :], r_recv)
        block = g_full[t]
        right = r_full[t]
        half_turn = dot(l_own[t], block, 0, 0).astype(BF16)
        rotated = dot(half_turn, right)
        moment = 0.95 * stat_m[t] + 0.05 * rotated * rotated
        new_moment_ref[t] = jnp.where(used[t] > 0.0, moment, stat_m[t])
        scaled = (rotated / (jnp.sqrt(moment) + epsilon)).astype(BF16)
        back_own[t] = dot(scaled, right, 1, 1).astype(BF16)
        for d in range(1, groups):
            p = x_peer(d)
            remote(
                back_own.at[t, :, column(p)], back_full.at[t, column(x), :],
                d_send, d_recv.at[t], (p, f),
            ).start()
        back_full[t, column(x), :] = back_own[t, :, column(x)]
    arrived(l_full.at[:, parts, :], l_recv)
    outs = []
    for t in range(2):
        arrived(back_full.at[t, parts, :], d_recv.at[t])
        outs.append(dot(l_full[t], back_full[t]).astype(BF16))
    half = chunk // 2
    for j in range(chips // per):
        both = jnp.concatenate([o[j * half : (j + 1) * half] for o in outs], axis=0)
        part = dot(sort_out[...], both).astype(BF16)
        out_own[j * half : (j + 1) * half] = part[:half]
        out_send[j * half : (j + 1) * half] = part[half:]
    share = remote(out_send, out_recv, y_send, y_recv, sibling)
    share.start()
    share.wait()
    near = out_own[...].astype(F32).reshape(chips, 2 * rows, LANES)
    away = out_recv[...].astype(F32).reshape(chips, 2 * rows, LANES)
    send_e[...] = jnp.concatenate([near, away], axis=1).astype(BF16)

    def step(i, carry):
        to = lax.rem(chip + i * 37, chips)
        remote(send_e.at[to], recv_e.at[chip], e_send, e_recv, (x, to * 2 + core)).start()
        return carry
    lax.fori_loop(1, chips, step, 0)
    recv_e[chip] = send_e[chip]
    for t in range(2):
        block = g_full[t]
        left_term = dot(g_full[t, column(x), :], block, 1, 1)
        new_left_ref[t] = jnp.where(used[t] > 0.0, 0.95 * stat_l[t] + 0.05 * left_term, stat_l[t])
        right_term = dot(g_full[t, :, column(x)], block, 0, 0)
        new_right_ref[t] = jnp.where(used[t] > 0.0, 0.95 * stat_r[t] + 0.05 * right_term, stat_r[t])
    arrived(recv_e.at[pl.ds(0, chips - 1)], e_recv)
    picked = dot(place[...], recv_e[...].reshape(chips * 4 * rows, LANES))
    update_ref[...] = picked.astype(BF16).reshape(layers, rows, blocks_per, LANES)

    arrived(raw.at[pl.ds(0, 3)], a_send)
    arrived(send_b.at[pl.ds(0, chips - 1)], b_send)
    arrived(send_e.at[pl.ds(0, chips - 1)], e_send)
    arrived(g_full.at[:, parts, :], c_send)
    arrived(r_full.at[:, parts, :], r_send)
    arrived(l_full.at[:, parts, :], l_send)
    arrived(back_full.at[:, parts, :], d_send)


def local(gradient, owner_slot, stat_left, stat_right, second_moment, basis_left, basis_right):
    layers, row_dev, columns = gradient.shape[1:]
    capacity, quarter, order = basis_right.shape
    blocks_per = columns // order
    chips = LINE * LINE
    many = layers * blocks_per * row_dev
    pieces = gradient.reshape(layers, row_dev, blocks_per, order)
    vmem = pl.BlockSpec(memory_space=pltpu.VMEM)
    anywhere = pl.BlockSpec(memory_space=pl.ANY)
    dma = pltpu.SemaphoreType.DMA
    message = (chips, 4 * row_dev, quarter)
    stat = (capacity, quarter, order)
    full = (capacity, order, order)
    return pl.pallas_call(
        kernel,
        name="soap_step",
        out_shape=(
            jax.ShapeDtypeStruct((layers, row_dev, blocks_per, quarter), BF16),
            jax.ShapeDtypeStruct(stat, F32),
            jax.ShapeDtypeStruct(stat, F32),
            jax.ShapeDtypeStruct(stat, F32),
        ),
        in_specs=[vmem, vmem] + [anywhere] * 5,
        out_specs=[vmem] * 4,
        scratch_shapes=[
            pltpu.VMEM((4, layers, row_dev, blocks_per, quarter), BF16),
            pltpu.VMEM((2, many, quarter), BF16),
            pltpu.VMEM((chips * 2 * row_dev, many), BF16),
            pltpu.VMEM((many, chips * 4 * row_dev), BF16),
            pltpu.VMEM((256, 256), BF16),
            pltpu.VMEM((256, 256), BF16),
            pltpu.VMEM(message, BF16),
            pltpu.VMEM(message, BF16),
            pltpu.VMEM(full, BF16),
            pltpu.VMEM(full, BF16),
            pltpu.VMEM(full, BF16),
            pltpu.VMEM((capacity, order, quarter), BF16),
            pltpu.VMEM((capacity, quarter, order), BF16),
            pltpu.VMEM((capacity, order, quarter), BF16),
            pltpu.VMEM((order, quarter), BF16),
            pltpu.VMEM((order, quarter), BF16),
            pltpu.VMEM((order, quarter), BF16),
            pltpu.VMEM(message, BF16),
            pltpu.VMEM(message, BF16),
            pltpu.VMEM(stat, F32),
            pltpu.VMEM(stat, F32),
            pltpu.VMEM(stat, F32),
            dma((9,)),
            dma, dma,
            dma, dma,
            dma, dma,
            dma, dma((2,)),
            dma, dma,
            dma, dma,
            dma, dma((2,)),
            dma, dma,
            dma, dma,
            pltpu.SemaphoreType.REGULAR,
        ],
        compiler_params=pltpu.CompilerParams(
            collective_id=0, has_side_effects=True, vmem_limit_bytes=40 << 20
        ),
    )(owner_slot, pieces, stat_left, stat_right, second_moment, basis_left, basis_right)


def solution(mesh):
    placed = (
        P("dp", None, "fsdp", None),
        P(),
        P("fsdp", "dp", None),
        P("fsdp", "dp", None),
        P("fsdp", "dp", None),
        P("fsdp", None, "dp"),
        P("fsdp", "dp", None),
    )
    return jax.shard_map(
        local,
        mesh=mesh,
        in_specs=placed,
        out_specs=(
            P(None, "fsdp", None, "dp"),
            P("fsdp", "dp", None),
            P("fsdp", "dp", None),
            P("fsdp", "dp", None),
        ),
        check_vma=False,
    )
```

```python
import functools

import jax
import jax.numpy as jnp
from jax import lax
from jax.experimental import pallas as pl
from jax.experimental.pallas import tpu as pltpu
from jax.sharding import PartitionSpec as P

epsilon = 1e-08
MESH = pl.DeviceIdType.MESH
F32, BF16, I32 = jnp.float32, jnp.bfloat16, jnp.int32
LINE = 8
LANES = 128


def iota(shape, dim):
    return lax.broadcasted_iota(I32, shape, dim)


def dot(a, b, ca=1, cb=0):
    return lax.dot_general(a, b, (((ca,), (cb,)), ((), ())), preferred_element_type=F32)


def one_hot(rows, columns):
    return jnp.where(rows == columns, 1.0, 0.0).astype(BF16)


def kernel(
    slot_ref, grad_ref, left_ref, right_ref, moment_ref, bl_ref, br_ref,
    update_ref, new_left_ref, new_right_ref, new_moment_ref,
    slot_vmem, raw, mean, pick, place, sort_in, sort_own, sort_sib,
    send_b, recv_b, g_full, l_full, r_full, l_own, back_own, back_full,
    out_own, out_sib, send_e, recv_e, stat_l, stat_r, stat_m, update,
    local_sem, store_sem, a_send, a_recv, x_send, x_recv, b_send, b_recv, c_send, c_recv,
    l_send, l_near, l_far, l_last, r_send, r_near, r_far, d_send, d_recv, y_send, y_recv,
    e_send, e_recv, tokens,
):
    x = lax.axis_index("dp")
    f = lax.axis_index("fsdp")
    groups = 4
    core = lax.rem(f, 2)
    chip = f // 2
    z, y = chip // LINE, lax.rem(chip, LINE)
    chips = LINE * LINE
    sibling = (x, f + 1 - 2 * core)
    layers, rows, blocks_per, _ = grad_ref.shape
    many = layers * rows * blocks_per
    order = g_full.shape[1]
    quarter = order // groups
    half = quarter // 2
    parts = pl.ds(0, order - quarter)

    def x_peer(d):
        return lax.rem(x + d + groups, groups)

    def device(zz, yy):
        return (x, (zz * LINE + yy) * 2 + core)

    def z_peer(d):
        return device(lax.rem(z + d + LINE, LINE), y)

    def y_peer(d):
        return device(z, lax.rem(y + d + LINE, LINE))

    def column(p):
        return pl.ds(pl.multiple_of(p * LANES, LANES), LANES)

    def row_half(p, size, which):
        return pl.ds(pl.multiple_of(p * size + which * (size // 2), size // 2), size // 2)

    def remote(src, dst, send, recv, to):
        return pltpu.make_async_remote_copy(
            src_ref=src, dst_ref=dst, send_sem=send, recv_sem=recv,
            device_id=to, device_id_type=MESH,
        )

    def signal(sem, to):
        pl.semaphore_signal(sem, inc=1, device_id=to, device_id_type=MESH)

    pending = {}

    def started(name, ref, sem):
        pending[name] = lambda: pltpu.make_async_copy(ref, ref, sem).wait()

    def arrived(name):
        pending.pop(name)()

    def finish():
        for name in list(pending):
            arrived(name)

    barrier = pltpu.get_barrier_semaphore()
    for d in (2, 1, -1):
        signal(barrier, (x_peer(d), f))
    for d in (1, -1):
        signal(barrier, z_peer(d))
        signal(barrier, y_peer(d))
    signal(barrier, sibling)

    loads = [
        pltpu.make_async_copy(slot_ref, slot_vmem, local_sem.at[0]),
        pltpu.make_async_copy(grad_ref.at[:, :, :, column(x)], raw.at[3], local_sem.at[1]),
        pltpu.make_async_copy(bl_ref, l_own, local_sem.at[2]),
        pltpu.make_async_copy(left_ref, stat_l, local_sem.at[3]),
        pltpu.make_async_copy(right_ref, stat_r, local_sem.at[4]),
        pltpu.make_async_copy(moment_ref, stat_m, local_sem.at[5]),
    ]
    for t in range(2):
        loads.append(pltpu.make_async_copy(bl_ref.at[t], l_full.at[t, :, column(x)], local_sem.at[6 + t]))
        loads.append(pltpu.make_async_copy(br_ref.at[t], r_full.at[t, column(x), :], local_sem.at[8 + t]))
    for i, load in enumerate(loads):
        load.start()
        pending["load", i] = load.wait
    pl.semaphore_wait(barrier, 8)

    for d in (2, 1, -1):
        p = x_peer(d)
        at = {2: 1, 1: 0, -1: 2}[d]
        remote(grad_ref.at[:, :, :, column(p)], raw.at[at], a_send, a_recv, (p, f)).start()
    started("groups", raw.at[pl.ds(0, 3)], a_recv)
    started("groups sent", raw.at[pl.ds(0, 3)], a_send)

    def greet(i, peers):
        for d in (1, -1):
            signal(tokens.at[i], peers(d * (2 if i in (1, 4) else 1)))
        pending["token", i] = lambda: pl.semaphore_wait(tokens.at[i], 2)

    greet(0, z_peer)

    arrived(("load", 0))
    slots = slot_vmem[...].astype(F32).astype(BF16)
    spread = one_hot(lax.rem(iota((blocks_per, many), 1), blocks_per), iota((blocks_per, many), 0))
    wide = dot(slots, spread)
    own_layer = iota((layers, many), 1) // (rows * blocks_per) == iota((layers, many), 0)
    slot_lane = jnp.sum(jnp.where(own_layer, wide, 0.0), axis=0, keepdims=True).astype(I32)
    row_lane = lax.rem(iota((1, many), 1) // blocks_per, rows)
    owner_lane = slot_lane // 2
    code_lane = jnp.where(
        lax.rem(owner_lane, 2) == core,
        (owner_lane // 2) * 2 * rows + lax.rem(slot_lane, 2) * rows + row_lane, -1,
    )
    used = [jnp.max(jnp.where(slot_lane == 2 * f + t, 1.0, 0.0), axis=1, keepdims=True) for t in range(2)]
    pick[...] = one_hot(code_lane, iota((chips * 2 * rows, many), 0))
    arrived(("token", 0))
    greet(1, z_peer)
    tall_spread = one_hot(lax.rem(iota((many, blocks_per), 0), blocks_per), iota((many, blocks_per), 1))
    tall = dot(tall_spread, slots, 1, 1)
    tall_layer = iota((many, layers), 0) // (rows * blocks_per) == iota((many, layers), 1)
    slot_col = jnp.sum(jnp.where(tall_layer, tall, 0.0), axis=1, keepdims=True).astype(I32)
    row_col = lax.rem(iota((many, 1), 0) // blocks_per, rows)
    owner_col = slot_col // 2
    far = jnp.where(lax.rem(owner_col, 2) == core, 0, 1)
    code_col = ((owner_col // 2) * 2 + far) * 2 * rows + lax.rem(slot_col, 2) * rows + row_col
    place[...] = one_hot(code_col, iota((many, chips * 4 * rows), 1))
    arrived(("token", 1))
    greet(2, y_peer)
    chunk = 256
    part = chunk // 2
    per = chunk // (4 * rows)
    ro, co = iota((chunk, 1), 0), iota((1, chunk), 1)
    far_o = lax.rem(lax.rem(ro // rows, 2) + core, 2)
    want = ((lax.rem(ro // (2 * rows), per) * 2 + far_o) * 2 + ro // part) * rows + lax.rem(ro, rows)
    sort_in[...] = one_hot(want, co)
    chip_o = ro // (4 * rows)
    t_o = lax.rem(ro // rows, 2)
    want = ((t_o * per + chip_o) * 2 + core) * rows + lax.rem(ro, rows)
    far_o = lax.rem(ro // (2 * rows), 2)
    sort_own[...] = one_hot(jnp.where(far_o == 0, want, -1), co)
    sort_sib[...] = one_hot(jnp.where(far_o == 1, want, -1), co)
    arrived(("token", 2))
    greet(3, y_peer)
    for i in range(1, len(loads)):
        arrived(("load", i))
    arrived(("token", 3))
    greet(4, y_peer)

    arrived("groups")
    total = raw[0].astype(F32) + raw[1].astype(F32) + raw[2].astype(F32) + raw[3].astype(F32)
    mean[0] = (total * (1.0 / groups)).astype(BF16).reshape(many, LANES)
    share = remote(mean.at[0], mean.at[1], x_send, x_recv, sibling)
    share.start()
    pending["mean"] = share.wait
    for t in range(2):
        for d in (1, -1):
            mine = r_full.at[t, column(x), :]
            remote(mine, mine, r_send, r_near, (x_peer(d), f)).start()
    for d in (1, -1):
        mine = l_full.at[0, :, column(x)]
        remote(mine, mine, l_send, l_near, (x_peer(d), f)).start()
    started("right near", r_full.at[:, pl.ds(0, 2 * quarter), :], r_near)
    started("right sent", r_full.at[:, pl.ds(0, 2 * quarter), :], r_send)
    started("left near", l_full.at[0, pl.ds(0, 2 * quarter), :], l_near)
    started("left sent", l_full.at[0, pl.ds(0, 2 * quarter), :], l_send)

    near = dot(pick[...], mean[0]).reshape(chips, 2 * rows, LANES)
    arrived("mean")
    away = dot(pick[...], mean[1]).reshape(chips, 2 * rows, LANES)
    send_b[...] = jnp.concatenate([near, away], axis=1).astype(BF16)

    arrived(("token", 4))

    def all_to_all(name, src, dst, send, recv):
        def step(i, carry):
            to = lax.rem(chip + i * 37, chips)
            remote(src.at[to], dst.at[chip], send, recv, (x, to * 2 + core)).start()
            return carry
        lax.fori_loop(1, chips, step, 0)
        dst[chip] = src[chip]
        started(name, dst.at[pl.ds(0, chips - 1)], recv)
        started(name + " sent", src.at[pl.ds(0, chips - 1)], send)

    all_to_all("rows", send_b, recv_b, b_send, b_recv)

    arrived("right near")
    for t in range(2):
        for i, d in enumerate((1, -1)):
            piece = r_full.at[t, row_half(x_peer(-d), quarter, i), :]
            remote(piece, piece, r_send, r_far, (x_peer(d), f)).start()
    started("right", r_full.at[:, pl.ds(0, quarter), :], r_far)
    started("right sent", r_full.at[:, parts, :], r_send)

    arrived("rows")
    for j in range(chips // per):
        rows_j = dot(sort_in[...], recv_b[j * per : (j + 1) * per].reshape(chunk, LANES)).astype(BF16)
        for t in range(2):
            g_full[t, j * part : (j + 1) * part, column(x)] = rows_j[t * part : (t + 1) * part]
    for t in range(2):
        for d in (2, 1, -1):
            mine = g_full.at[t, :, column(x)]
            remote(mine, mine, c_send, c_recv.at[t], (x_peer(d), f)).start()
        started(("block", t), g_full.at[t, parts, :], c_recv.at[t])
    started("blocks sent", g_full.at[:, parts, :], c_send)
    arrived("left near")
    for i, d in enumerate((1, -1)):
        piece = l_full.at[0, pl.ds(i * (order // 2), order // 2), column(x_peer(-d))]
        remote(piece, piece, l_send, l_far, (x_peer(d), f)).start()
    started("left 0", l_full.at[0, pl.ds(0, quarter), :], l_far)
    started("left sent", l_full.at[0, parts, :], l_send)
    arrived("right")

    def block_step(t):
        block = g_full[t]
        right = r_full[t]
        half_turn = dot(l_own[t], block, 0, 0).astype(BF16)
        rotated = dot(half_turn, right)
        moment = 0.95 * stat_m[t] + 0.05 * rotated * rotated
        stat_m[t] = jnp.where(used[t] > 0.0, moment, stat_m[t])
        scaled = (rotated / (jnp.sqrt(moment) + epsilon)).astype(BF16)
        back_own[t] = dot(scaled, right, 1, 1).astype(BF16)
        for d in (2, 1, -1):
            p = x_peer(d)
            remote(
                back_own.at[t, :, column(p)], back_full.at[t, column(x), :],
                d_send, d_recv.at[t], (p, f),
            ).start()
        started(("back", t), back_full.at[t, parts, :], d_recv.at[t])
        started("back sent", back_full.at[pl.ds(0, t + 1), parts, :], d_send)
        back_full[t, column(x), :] = back_own[t, :, column(x)]

    def out_step(t):
        arrived(("back", t))
        out_own[t] = dot(l_full[t], back_full[t]).astype(BF16)
        remote(out_own.at[t], out_sib.at[t], y_send, y_recv.at[t], sibling).start()
        started(("out", t), out_sib.at[t], y_recv.at[t])
        started("out sent", out_own.at[pl.ds(0, t + 1)], y_send)

    arrived(("block", 0))
    block_step(0)
    arrived(("block", 1))
    for d in (2, 1, -1):
        mine = l_full.at[1, :, column(x)]
        remote(mine, mine, l_send, l_last, (x_peer(d), f)).start()
    started("left 1", l_full.at[1, parts, :], l_last)
    started("left sent", l_full.at[:, parts, :], l_send)
    block_step(1)
    arrived("left 0")
    out_step(0)
    arrived("left 1")
    out_step(1)
    def sort_rows(ref, sort, j):
        both = jnp.concatenate([ref[t, j * part : (j + 1) * part] for t in range(2)], axis=0)
        return dot(sort[...], both)

    mine = [sort_rows(out_own, sort_own, j) for j in range(chips // per)]
    arrived(("out", 0))
    arrived(("out", 1))
    for j in range(chips // per):
        both = (mine[j] + sort_rows(out_sib, sort_sib, j)).astype(BF16)
        send_e[j * per : (j + 1) * per] = both.reshape(per, 4 * rows, LANES)

    all_to_all("update", send_e, recv_e, e_send, e_recv)
    stores = []

    def store(src, dst):
        copy = pltpu.make_async_copy(src, dst, store_sem.at[len(stores)])
        copy.start()
        pending["store", len(stores)] = copy.wait
        stores.append(copy)

    store(stat_m, new_moment_ref)
    for t in range(2):
        block = g_full[t]
        left_term = dot(g_full[t, column(x), :], block, 1, 1)
        stat_l[t] = jnp.where(used[t] > 0.0, 0.95 * stat_l[t] + 0.05 * left_term, stat_l[t])
        store(stat_l.at[t], new_left_ref.at[t])
        right_term = dot(g_full[t, :, column(x)], block, 0, 0)
        stat_r[t] = jnp.where(used[t] > 0.0, 0.95 * stat_r[t] + 0.05 * right_term, stat_r[t])
        store(stat_r.at[t], new_right_ref.at[t])
    arrived("update")
    picked = dot(place[...], recv_e[...].reshape(chips * 4 * rows, LANES))
    update[...] = picked.astype(BF16).reshape(layers, rows, blocks_per, LANES)
    store(update, update_ref)
    finish()


def store_kernel(*refs):
    count = len(refs) // 3
    semaphores = refs[-1]
    moves = [
        (
            pltpu.make_async_copy(refs[i], refs[2 * count + i], semaphores.at[i]),
            pltpu.make_async_copy(refs[2 * count + i], refs[count + i], semaphores.at[count + i]),
        )
        for i in range(count)
    ]
    for load, _ in moves:
        load.start()
    for load, store in moves:
        load.wait()
        store.start()
    for _, store in moves:
        store.wait()


def local(gradient, owner_slot, stat_left, stat_right, second_moment, basis_left, basis_right):
    layers, row_dev, columns = gradient.shape[1:]
    capacity, quarter, order = basis_right.shape
    blocks_per = columns // order
    chips = LINE * LINE
    many = layers * blocks_per * row_dev
    pieces = gradient.reshape(layers, row_dev, blocks_per, order)
    hbm = pl.BlockSpec(memory_space=pltpu.HBM)
    dma = pltpu.SemaphoreType.DMA
    message = (chips, 4 * row_dev, quarter)
    stat = (capacity, quarter, order)
    full = (capacity, order, order)
    results = pl.pallas_call(
        kernel,
        name="soap_step",
        out_shape=(
            jax.ShapeDtypeStruct((layers, row_dev, blocks_per, quarter), BF16),
            jax.ShapeDtypeStruct(stat, F32),
            jax.ShapeDtypeStruct(stat, F32),
            jax.ShapeDtypeStruct(stat, F32),
        ),
        in_specs=[hbm] * 7,
        out_specs=[hbm] * 4,
        scratch_shapes=[
            pltpu.VMEM(owner_slot.shape, I32),
            pltpu.VMEM((4, layers, row_dev, blocks_per, quarter), BF16),
            pltpu.VMEM((2, many, quarter), BF16),
            pltpu.VMEM((chips * 2 * row_dev, many), BF16),
            pltpu.VMEM((many, chips * 4 * row_dev), BF16),
            pltpu.VMEM((256, 256), BF16),
            pltpu.VMEM((256, 256), BF16),
            pltpu.VMEM((256, 256), BF16),
            pltpu.VMEM(message, BF16),
            pltpu.VMEM(message, BF16),
            pltpu.VMEM(full, BF16),
            pltpu.VMEM(full, BF16),
            pltpu.VMEM(full, BF16),
            pltpu.VMEM((capacity, order, quarter), BF16),
            pltpu.VMEM((capacity, quarter, order), BF16),
            pltpu.VMEM((capacity, order, quarter), BF16),
            pltpu.VMEM((capacity, order, quarter), BF16),
            pltpu.VMEM((capacity, order, quarter), BF16),
            pltpu.VMEM(message, BF16),
            pltpu.VMEM(message, BF16),
            pltpu.VMEM(stat, F32),
            pltpu.VMEM(stat, F32),
            pltpu.VMEM(stat, F32),
            pltpu.VMEM((layers, row_dev, blocks_per, quarter), BF16),
            dma((10,)),
            dma((6,)),
            dma, dma,
            dma, dma,
            dma, dma,
            dma, dma((2,)),
            dma, dma, dma, dma,
            dma, dma, dma,
            dma, dma((2,)),
            dma, dma((2,)),
            dma, dma,
            pltpu.SemaphoreType.REGULAR((5,)),
        ],
        compiler_params=pltpu.CompilerParams(
            collective_id=0, has_side_effects=True, vmem_limit_bytes=60 << 20
        ),
    )(owner_slot, pieces, stat_left, stat_right, second_moment, basis_left, basis_right)
    return pl.pallas_call(
        store_kernel,
        name="store",
        out_shape=tuple(jax.ShapeDtypeStruct(r.shape, r.dtype) for r in results),
        in_specs=[hbm] * 4,
        out_specs=[hbm] * 4,
        scratch_shapes=[pltpu.VMEM(r.shape, r.dtype) for r in results] + [dma((8,))],
        compiler_params=pltpu.CompilerParams(vmem_limit_bytes=60 << 20),
    )(*results)


def solution(mesh):
    placed = (
        P("dp", None, "fsdp", None),
        P(),
        P("fsdp", "dp", None),
        P("fsdp", "dp", None),
        P("fsdp", "dp", None),
        P("fsdp", None, "dp"),
        P("fsdp", "dp", None),
    )
    return jax.shard_map(
        local,
        mesh=mesh,
        in_specs=placed,
        out_specs=(
            P(None, "fsdp", None, "dp"),
            P("fsdp", "dp", None),
            P("fsdp", "dp", None),
            P("fsdp", "dp", None),
        ),
        check_vma=False,
    )
```

```python
import functools

import jax
import jax.numpy as jnp
from jax import lax
from jax.experimental import pallas as pl
from jax.experimental.pallas import tpu as pltpu
from jax.sharding import PartitionSpec as P

epsilon = 1e-08
MESH = pl.DeviceIdType.MESH
F32, BF16, I32 = jnp.float32, jnp.bfloat16, jnp.int32
LINE = 8
LANES = 128


def hops(d):
    return min(d, LINE - d)


far_first = sorted(
    ((dz, dy) for dz in range(LINE) for dy in range(LINE) if dz or dy),
    key=lambda step: -hops(step[0]) - hops(step[1]),
)


def iota(shape, dim):
    return lax.broadcasted_iota(I32, shape, dim)


def dot(a, b, ca=1, cb=0):
    return lax.dot_general(a, b, (((ca,), (cb,)), ((), ())), preferred_element_type=F32)


def one_hot(rows, columns):
    return jnp.where(rows == columns, 1.0, 0.0).astype(BF16)


def kernel(
    slot_ref, grad_ref, left_ref, right_ref, moment_ref, bl_ref, br_ref,
    update_ref, new_left_ref, new_right_ref, new_moment_ref,
    slot_vmem, raw, mean, pick, place, sort_in, sort_own, sort_sib,
    send_b, recv_b, g_full, l_full, r_full, l_own, back_own, back_full,
    out_own, out_sib, send_e, recv_e, stat_l, stat_r, stat_m,
    local_sem, a_send, a_recv, x_send, x_recv, b_send, b_recv, c_send, c_near, c_far,
    l_send, l_near, l_far, l_last, r_send, r_near, r_far, d_send, d_recv, y_send, y_recv,
    e_send, e_recv, tokens,
):
    x = lax.axis_index("dp")
    f = lax.axis_index("fsdp")
    groups = 4
    core = lax.rem(f, 2)
    chip = f // 2
    z, y = chip // LINE, lax.rem(chip, LINE)
    chips = LINE * LINE
    sibling = (x, f + 1 - 2 * core)
    layers, rows, blocks_per, _ = grad_ref.shape
    many = layers * rows * blocks_per
    order = g_full.shape[1]
    quarter = order // groups
    half = quarter // 2
    parts = pl.ds(0, order - quarter)

    def x_peer(d):
        return lax.rem(x + d + groups, groups)

    def device(zz, yy):
        return (x, (zz * LINE + yy) * 2 + core)

    def z_peer(d):
        return device(lax.rem(z + d + LINE, LINE), y)

    def y_peer(d):
        return device(z, lax.rem(y + d + LINE, LINE))

    def column(p):
        return pl.ds(pl.multiple_of(p * LANES, LANES), LANES)

    def row_half(p, size, which):
        return pl.ds(pl.multiple_of(p * size + which * (size // 2), size // 2), size // 2)

    def remote(src, dst, send, recv, to):
        return pltpu.make_async_remote_copy(
            src_ref=src, dst_ref=dst, send_sem=send, recv_sem=recv,
            device_id=to, device_id_type=MESH,
        )

    def signal(sem, to):
        pl.semaphore_signal(sem, inc=1, device_id=to, device_id_type=MESH)

    pending = {}

    def started(name, ref, sem):
        pending[name] = lambda: pltpu.make_async_copy(ref, ref, sem).wait()

    def arrived(name):
        pending.pop(name)()

    def finish():
        for name in list(pending):
            arrived(name)

    barrier = pltpu.get_barrier_semaphore()
    for d in (2, 1, -1):
        signal(barrier, (x_peer(d), f))
    for d in (1, -1):
        signal(barrier, z_peer(d))
        signal(barrier, y_peer(d))
    signal(barrier, sibling)

    loads = [
        pltpu.make_async_copy(slot_ref, slot_vmem, local_sem.at[0]),
        pltpu.make_async_copy(grad_ref.at[:, :, :, column(x)], raw.at[3], local_sem.at[1]),
        pltpu.make_async_copy(bl_ref, l_own, local_sem.at[2]),
        pltpu.make_async_copy(left_ref, stat_l, local_sem.at[3]),
        pltpu.make_async_copy(right_ref, stat_r, local_sem.at[4]),
        pltpu.make_async_copy(moment_ref, stat_m, local_sem.at[5]),
    ]
    for t in range(2):
        loads.append(pltpu.make_async_copy(bl_ref.at[t], l_full.at[t, :, column(x)], local_sem.at[6 + t]))
        loads.append(pltpu.make_async_copy(br_ref.at[t], r_full.at[t, column(x), :], local_sem.at[8 + t]))
    for i, load in enumerate(loads):
        load.start()
        pending["load", i] = load.wait
    pl.semaphore_wait(barrier, 8)

    for d in (2, 1, -1):
        p = x_peer(d)
        at = {2: 1, 1: 0, -1: 2}[d]
        remote(grad_ref.at[:, :, :, column(p)], raw.at[at], a_send, a_recv, (p, f)).start()
    started("groups", raw.at[pl.ds(0, 3)], a_recv)
    started("groups sent", raw.at[pl.ds(0, 3)], a_send)

    def greet(i, peers):
        for d in (1, -1):
            signal(tokens.at[i], peers(d * (2 if i in (1, 4) else 1)))
        pending["token", i] = lambda: pl.semaphore_wait(tokens.at[i], 2)

    greet(0, z_peer)

    arrived(("load", 0))
    slots = slot_vmem[...].astype(F32).astype(BF16)
    spread = one_hot(lax.rem(iota((blocks_per, many), 1), blocks_per), iota((blocks_per, many), 0))
    wide = dot(slots, spread)
    own_layer = iota((layers, many), 1) // (rows * blocks_per) == iota((layers, many), 0)
    slot_lane = jnp.sum(jnp.where(own_layer, wide, 0.0), axis=0, keepdims=True).astype(I32)
    row_lane = lax.rem(iota((1, many), 1) // blocks_per, rows)
    owner_lane = slot_lane // 2
    code_lane = jnp.where(
        lax.rem(owner_lane, 2) == core,
        (owner_lane // 2) * 2 * rows + lax.rem(slot_lane, 2) * rows + row_lane, -1,
    )
    used = [jnp.max(jnp.where(slot_lane == 2 * f + t, 1.0, 0.0), axis=1, keepdims=True) for t in range(2)]
    pick[...] = one_hot(code_lane, iota((chips * 2 * rows, many), 0))
    arrived(("token", 0))
    greet(1, z_peer)
    tall_spread = one_hot(lax.rem(iota((many, blocks_per), 0), blocks_per), iota((many, blocks_per), 1))
    tall = dot(tall_spread, slots, 1, 1)
    tall_layer = iota((many, layers), 0) // (rows * blocks_per) == iota((many, layers), 1)
    slot_col = jnp.sum(jnp.where(tall_layer, tall, 0.0), axis=1, keepdims=True).astype(I32)
    row_col = lax.rem(iota((many, 1), 0) // blocks_per, rows)
    owner_col = slot_col // 2
    far = jnp.where(lax.rem(owner_col, 2) == core, 0, 1)
    code_col = ((owner_col // 2) * 2 + far) * 2 * rows + lax.rem(slot_col, 2) * rows + row_col
    place[...] = one_hot(code_col, iota((many, chips * 4 * rows), 1))
    arrived(("token", 1))
    greet(2, y_peer)
    chunk = 256
    part = chunk // 2
    per = chunk // (4 * rows)
    ro, co = iota((chunk, 1), 0), iota((1, chunk), 1)
    far_o = lax.rem(lax.rem(ro // rows, 2) + core, 2)
    want = ((lax.rem(ro // (2 * rows), per) * 2 + far_o) * 2 + ro // part) * rows + lax.rem(ro, rows)
    sort_in[...] = one_hot(want, co)
    chip_o = ro // (4 * rows)
    t_o = lax.rem(ro // rows, 2)
    want = ((t_o * per + chip_o) * 2 + core) * rows + lax.rem(ro, rows)
    far_o = lax.rem(ro // (2 * rows), 2)
    sort_own[...] = one_hot(jnp.where(far_o == 0, want, -1), co)
    sort_sib[...] = one_hot(jnp.where(far_o == 1, want, -1), co)
    arrived(("token", 2))
    greet(3, y_peer)
    for i in range(1, len(loads)):
        arrived(("load", i))
    arrived(("token", 3))
    greet(4, y_peer)

    arrived("groups")
    total = raw[0].astype(F32) + raw[1].astype(F32) + raw[2].astype(F32) + raw[3].astype(F32)
    mean[0] = (total * (1.0 / groups)).astype(BF16).reshape(many, LANES)
    share = remote(mean.at[0], mean.at[1], x_send, x_recv, sibling)
    share.start()
    pending["mean"] = share.wait
    for t in range(2):
        for d in (1, -1):
            mine = r_full.at[t, column(x), :]
            remote(mine, mine, r_send, r_near, (x_peer(d), f)).start()
    for d in (1, -1):
        mine = l_full.at[0, :, column(x)]
        remote(mine, mine, l_send, l_near, (x_peer(d), f)).start()
    started("right near", r_full.at[:, pl.ds(0, 2 * quarter), :], r_near)
    started("right sent", r_full.at[:, pl.ds(0, 2 * quarter), :], r_send)
    started("left near", l_full.at[0, pl.ds(0, 2 * quarter), :], l_near)
    started("left sent", l_full.at[0, pl.ds(0, 2 * quarter), :], l_send)

    near = dot(pick[...], mean[0]).reshape(chips, 2 * rows, LANES)
    arrived("mean")
    away = dot(pick[...], mean[1]).reshape(chips, 2 * rows, LANES)
    send_b[...] = jnp.concatenate([near, away], axis=1).astype(BF16)

    arrived(("token", 4))

    along_z = [lax.rem(z + d, LINE) for d in range(LINE)]
    along_y = [lax.rem(y + d, LINE) for d in range(LINE)]

    def all_to_all(name, src, dst, send, recv):
        for dz, dy in far_first:
            to = along_z[dz] * LINE + along_y[dy]
            remote(src.at[to], dst.at[chip], send, recv, (x, to * 2 + core)).start()
        dst[chip] = src[chip]
        started(name, dst.at[pl.ds(0, chips - 1)], recv)
        started(name + " sent", src.at[pl.ds(0, chips - 1)], send)

    all_to_all("rows", send_b, recv_b, b_send, b_recv)

    arrived("right near")
    for t in range(2):
        for i, d in enumerate((1, -1)):
            piece = r_full.at[t, row_half(x_peer(-d), quarter, i), :]
            remote(piece, piece, r_send, r_far, (x_peer(d), f)).start()
    started("right", r_full.at[:, pl.ds(0, quarter), :], r_far)
    started("right sent", r_full.at[:, parts, :], r_send)

    arrived("left near")
    for i, d in enumerate((1, -1)):
        piece = l_full.at[0, pl.ds(i * (order // 2), order // 2), column(x_peer(-d))]
        remote(piece, piece, l_send, l_far, (x_peer(d), f)).start()
    started("left 0", l_full.at[0, pl.ds(0, quarter), :], l_far)
    started("left sent", l_full.at[0, parts, :], l_send)

    arrived("rows")
    for j in range(chips // per):
        rows_j = dot(sort_in[...], recv_b[j * per : (j + 1) * per].reshape(chunk, LANES)).astype(BF16)
        for t in range(2):
            g_full[t, j * part : (j + 1) * part, column(x)] = rows_j[t * part : (t + 1) * part]
    for t in range(2):
        for d in (1, -1):
            mine = g_full.at[t, :, column(x)]
            remote(mine, mine, c_send, c_near.at[t], (x_peer(d), f)).start()
        started(("block near", t), g_full.at[t, pl.ds(0, 2 * quarter), :], c_near.at[t])
    started("blocks sent", g_full.at[:, pl.ds(0, 2 * quarter), :], c_send)
    for t in range(2):
        arrived(("block near", t))
        for i, d in enumerate((1, -1)):
            piece = g_full.at[t, pl.ds(i * (order // 2), order // 2), column(x_peer(-d))]
            remote(piece, piece, c_send, c_far.at[t], (x_peer(d), f)).start()
        started(("block", t), g_full.at[t, pl.ds(0, quarter), :], c_far.at[t])
    started("blocks sent", g_full.at[:, parts, :], c_send)
    for d in (2, 1, -1):
        mine = l_full.at[1, :, column(x)]
        remote(mine, mine, l_send, l_last, (x_peer(d), f)).start()
    started("left 1", l_full.at[1, parts, :], l_last)
    started("left sent", l_full.at[:, parts, :], l_send)
    arrived("right")

    def block_step(t):
        block = g_full[t]
        right = r_full[t]
        half_turn = dot(l_own[t], block, 0, 0).astype(BF16)
        rotated = dot(half_turn, right)
        moment = 0.95 * stat_m[t] + 0.05 * rotated * rotated
        new_moment_ref[t] = jnp.where(used[t] > 0.0, moment, stat_m[t])
        scaled = (rotated / (jnp.sqrt(moment) + epsilon)).astype(BF16)
        back_own[t] = dot(scaled, right, 1, 1).astype(BF16)
        for d in (2, 1, -1):
            p = x_peer(d)
            remote(
                back_own.at[t, :, column(p)], back_full.at[t, column(x), :],
                d_send, d_recv.at[t], (p, f),
            ).start()
        started(("back", t), back_full.at[t, parts, :], d_recv.at[t])
        started("back sent", back_full.at[pl.ds(0, t + 1), parts, :], d_send)
        back_full[t, column(x), :] = back_own[t, :, column(x)]

    def out_step(t):
        arrived(("back", t))
        out_own[t] = dot(l_full[t], back_full[t]).astype(BF16)
        remote(out_own.at[t], out_sib.at[t], y_send, y_recv.at[t], sibling).start()
        started(("out", t), out_sib.at[t], y_recv.at[t])
        started("out sent", out_own.at[pl.ds(0, t + 1)], y_send)

    arrived(("block", 0))
    block_step(0)
    arrived(("block", 1))
    block_step(1)
    arrived("left 0")
    out_step(0)
    arrived("left 1")
    out_step(1)
    def sort_rows(ref, sort, j):
        both = jnp.concatenate([ref[t, j * part : (j + 1) * part] for t in range(2)], axis=0)
        return dot(sort[...], both)

    mine = [sort_rows(out_own, sort_own, j) for j in range(chips // per)]
    arrived(("out", 0))
    arrived(("out", 1))
    for j in range(chips // per):
        both = (mine[j] + sort_rows(out_sib, sort_sib, j)).astype(BF16)
        send_e[j * per : (j + 1) * per] = both.reshape(per, 4 * rows, LANES)

    all_to_all("update", send_e, recv_e, e_send, e_recv)
    for t in range(2):
        block = g_full[t]
        left_term = dot(g_full[t, column(x), :], block, 1, 1)
        new_left_ref[t] = jnp.where(used[t] > 0.0, 0.95 * stat_l[t] + 0.05 * left_term, stat_l[t])
        right_term = dot(g_full[t, :, column(x)], block, 0, 0)
        new_right_ref[t] = jnp.where(used[t] > 0.0, 0.95 * stat_r[t] + 0.05 * right_term, stat_r[t])
    arrived("update")
    picked = dot(place[...], recv_e[...].reshape(chips * 4 * rows, LANES))
    update_ref[...] = picked.astype(BF16).reshape(layers, rows, blocks_per, LANES)
    finish()


def stay(array):
    return pltpu.with_memory_space_constraint(array, pltpu.HBM)


def store_kernel(*refs):
    count = (len(refs) - 1) // 2
    copies = [
        pltpu.make_async_copy(refs[i], refs[count + i], refs[-1].at[i]) for i in range(count)
    ]
    for copy in copies:
        copy.start()
    for copy in copies:
        copy.wait()


def local(gradient, owner_slot, stat_left, stat_right, second_moment, basis_left, basis_right):
    layers, row_dev, columns = gradient.shape[1:]
    capacity, quarter, order = basis_right.shape
    blocks_per = columns // order
    chips = LINE * LINE
    many = layers * blocks_per * row_dev
    pieces = gradient.reshape(layers, row_dev, blocks_per, order)
    vmem = pl.BlockSpec(memory_space=pltpu.VMEM)
    hbm = pl.BlockSpec(memory_space=pltpu.HBM)
    dma = pltpu.SemaphoreType.DMA
    message = (chips, 4 * row_dev, quarter)
    stat = (capacity, quarter, order)
    full = (capacity, order, order)
    results = pl.pallas_call(
        kernel,
        name="soap_step",
        out_shape=(
            pltpu.VMEM((layers, row_dev, blocks_per, quarter), BF16),
            pltpu.VMEM(stat, F32),
            pltpu.VMEM(stat, F32),
            pltpu.VMEM(stat, F32),
        ),
        in_specs=[hbm, pl.BlockSpec(memory_space=pl.ANY)] + [hbm] * 5,
        out_specs=[vmem] * 4,
        scratch_shapes=[
            pltpu.VMEM(owner_slot.shape, I32),
            pltpu.VMEM((4, layers, row_dev, blocks_per, quarter), BF16),
            pltpu.VMEM((2, many, quarter), BF16),
            pltpu.VMEM((chips * 2 * row_dev, many), BF16),
            pltpu.VMEM((many, chips * 4 * row_dev), BF16),
            pltpu.VMEM((256, 256), BF16),
            pltpu.VMEM((256, 256), BF16),
            pltpu.VMEM((256, 256), BF16),
            pltpu.VMEM(message, BF16),
            pltpu.VMEM(message, BF16),
            pltpu.VMEM(full, BF16),
            pltpu.VMEM(full, BF16),
            pltpu.VMEM(full, BF16),
            pltpu.VMEM((capacity, order, quarter), BF16),
            pltpu.VMEM((capacity, quarter, order), BF16),
            pltpu.VMEM((capacity, order, quarter), BF16),
            pltpu.VMEM((capacity, order, quarter), BF16),
            pltpu.VMEM((capacity, order, quarter), BF16),
            pltpu.VMEM(message, BF16),
            pltpu.VMEM(message, BF16),
            pltpu.VMEM(stat, F32),
            pltpu.VMEM(stat, F32),
            pltpu.VMEM(stat, F32),
            dma((10,)),
            dma, dma,
            dma, dma,
            dma, dma,
            dma, dma((2,)), dma((2,)),
            dma, dma, dma, dma,
            dma, dma, dma,
            dma, dma((2,)),
            dma, dma((2,)),
            dma, dma,
            pltpu.SemaphoreType.REGULAR((5,)),
        ],
        compiler_params=pltpu.CompilerParams(
            collective_id=0, has_side_effects=True, vmem_limit_bytes=40 << 20
        ),
    )(stay(owner_slot), pieces, *(stay(a) for a in (stat_left, stat_right, second_moment, basis_left, basis_right)))
    return pl.pallas_call(
        store_kernel,
        name="store",
        out_shape=tuple(jax.ShapeDtypeStruct(r.shape, r.dtype) for r in results),
        in_specs=[vmem] * 4,
        out_specs=[hbm] * 4,
        scratch_shapes=[dma((4,))],
        compiler_params=pltpu.CompilerParams(vmem_limit_bytes=8 << 20),
    )(*results)


def solution(mesh):
    placed = (
        P("dp", None, "fsdp", None),
        P(),
        P("fsdp", "dp", None),
        P("fsdp", "dp", None),
        P("fsdp", "dp", None),
        P("fsdp", None, "dp"),
        P("fsdp", "dp", None),
    )
    return jax.shard_map(
        local,
        mesh=mesh,
        in_specs=placed,
        out_specs=(
            P(None, "fsdp", None, "dp"),
            P("fsdp", "dp", None),
            P("fsdp", "dp", None),
            P("fsdp", "dp", None),
        ),
        check_vma=False,
    )
```

```python
import functools

import jax
import jax.numpy as jnp
from jax import lax
from jax.experimental import pallas as pl
from jax.experimental.pallas import tpu as pltpu
from jax.sharding import PartitionSpec as P

epsilon = 1e-08
MESH = pl.DeviceIdType.MESH
F32, BF16, I32 = jnp.float32, jnp.bfloat16, jnp.int32
LINE = 8
LANES = 128


def hops(d):
    return min(d, LINE - d)


far_first = sorted(
    ((dz, dy) for dz in range(LINE) for dy in range(LINE) if dz or dy),
    key=lambda step: -hops(step[0]) - hops(step[1]),
)


def iota(shape, dim):
    return lax.broadcasted_iota(I32, shape, dim)


def dot(a, b, ca=1, cb=0):
    return lax.dot_general(a, b, (((ca,), (cb,)), ((), ())), preferred_element_type=F32)


def one_hot(rows, columns):
    return jnp.where(rows == columns, 1.0, 0.0).astype(BF16)


def kernel(
    slot_ref, grad_ref, left_ref, right_ref, moment_ref, bl_ref, br_ref,
    update_ref, new_left_ref, new_right_ref, new_moment_ref,
    slot_vmem, raw, mean, pick, place, sort_in, sort_own, sort_sib,
    send_b, recv_b, g_full, l_full, r_full, l_own, back_own, back_full,
    out_own, out_sib, send_e, recv_e, stat_l, stat_r, stat_m,
    local_sem, a_send, a_recv, x_send, x_recv, b_send, b_recv, c_send, c_near, c_far,
    l_send, l_near, l_far, r_send, r_near, r_far, d_send, d_recv, y_send, y_recv,
    e_send, e_recv, tokens,
):
    x = lax.axis_index("dp")
    f = lax.axis_index("fsdp")
    groups = 4
    core = lax.rem(f, 2)
    chip = f // 2
    z, y = chip // LINE, lax.rem(chip, LINE)
    chips = LINE * LINE
    sibling = (x, f + 1 - 2 * core)
    layers, rows, blocks_per, _ = grad_ref.shape
    many = layers * rows * blocks_per
    order = g_full.shape[1]
    quarter = order // groups
    half = quarter // 2
    parts = pl.ds(0, order - quarter)

    def x_peer(d):
        return lax.rem(x + d + groups, groups)

    def device(zz, yy):
        return (x, (zz * LINE + yy) * 2 + core)

    def z_peer(d):
        return device(lax.rem(z + d + LINE, LINE), y)

    def y_peer(d):
        return device(z, lax.rem(y + d + LINE, LINE))

    def column(p):
        return pl.ds(pl.multiple_of(p * LANES, LANES), LANES)

    def row_half(p, size, which):
        return pl.ds(pl.multiple_of(p * size + which * (size // 2), size // 2), size // 2)

    def remote(src, dst, send, recv, to):
        return pltpu.make_async_remote_copy(
            src_ref=src, dst_ref=dst, send_sem=send, recv_sem=recv,
            device_id=to, device_id_type=MESH,
        )

    def signal(sem, to):
        pl.semaphore_signal(sem, inc=1, device_id=to, device_id_type=MESH)

    pending = {}

    def started(name, ref, sem):
        pending[name] = lambda: pltpu.make_async_copy(ref, ref, sem).wait()

    def arrived(name):
        pending.pop(name)()

    def finish():
        for name in list(pending):
            arrived(name)

    barrier = pltpu.get_barrier_semaphore()
    for d in (2, 1, -1):
        signal(barrier, (x_peer(d), f))
    for d in (1, -1):
        signal(barrier, z_peer(d))
        signal(barrier, y_peer(d))
    signal(barrier, sibling)

    loads = [
        pltpu.make_async_copy(slot_ref, slot_vmem, local_sem.at[0]),
        pltpu.make_async_copy(grad_ref.at[:, :, :, column(x)], raw.at[3], local_sem.at[1]),
        pltpu.make_async_copy(bl_ref, l_own, local_sem.at[2]),
        pltpu.make_async_copy(left_ref, stat_l, local_sem.at[3]),
        pltpu.make_async_copy(right_ref, stat_r, local_sem.at[4]),
        pltpu.make_async_copy(moment_ref, stat_m, local_sem.at[5]),
    ]
    for t in range(2):
        loads.append(pltpu.make_async_copy(bl_ref.at[t], l_full.at[t, :, column(x)], local_sem.at[6 + t]))
        loads.append(pltpu.make_async_copy(br_ref.at[t], r_full.at[t, column(x), :], local_sem.at[8 + t]))
    for i, load in enumerate(loads):
        load.start()
        pending["load", i] = load.wait
    pl.semaphore_wait(barrier, 8)

    for d in (2, 1, -1):
        p = x_peer(d)
        at = {2: 1, 1: 0, -1: 2}[d]
        remote(grad_ref.at[:, :, :, column(p)], raw.at[at], a_send, a_recv, (p, f)).start()
    started("groups", raw.at[pl.ds(0, 3)], a_recv)
    started("groups sent", raw.at[pl.ds(0, 3)], a_send)

    def greet(i, peers):
        for d in (1, -1):
            signal(tokens.at[i], peers(d * (2 if i in (1, 4) else 1)))
        pending["token", i] = lambda: pl.semaphore_wait(tokens.at[i], 2)

    greet(0, z_peer)

    arrived(("load", 0))
    slots = slot_vmem[...].astype(F32).astype(BF16)
    spread = one_hot(lax.rem(iota((blocks_per, many), 1), blocks_per), iota((blocks_per, many), 0))
    wide = dot(slots, spread)
    own_layer = iota((layers, many), 1) // (rows * blocks_per) == iota((layers, many), 0)
    slot_lane = jnp.sum(jnp.where(own_layer, wide, 0.0), axis=0, keepdims=True).astype(I32)
    row_lane = lax.rem(iota((1, many), 1) // blocks_per, rows)
    owner_lane = slot_lane // 2
    code_lane = jnp.where(
        lax.rem(owner_lane, 2) == core,
        (owner_lane // 2) * 2 * rows + lax.rem(slot_lane, 2) * rows + row_lane, -1,
    )
    used = [jnp.max(jnp.where(slot_lane == 2 * f + t, 1.0, 0.0), axis=1, keepdims=True) for t in range(2)]
    pick[...] = one_hot(code_lane, iota((chips * 2 * rows, many), 0))
    arrived(("token", 0))
    greet(1, z_peer)
    tall_spread = one_hot(lax.rem(iota((many, blocks_per), 0), blocks_per), iota((many, blocks_per), 1))
    tall = dot(tall_spread, slots, 1, 1)
    tall_layer = iota((many, layers), 0) // (rows * blocks_per) == iota((many, layers), 1)
    slot_col = jnp.sum(jnp.where(tall_layer, tall, 0.0), axis=1, keepdims=True).astype(I32)
    row_col = lax.rem(iota((many, 1), 0) // blocks_per, rows)
    owner_col = slot_col // 2
    far = jnp.where(lax.rem(owner_col, 2) == core, 0, 1)
    code_col = ((owner_col // 2) * 2 + far) * 2 * rows + lax.rem(slot_col, 2) * rows + row_col
    place[...] = one_hot(code_col, iota((many, chips * 4 * rows), 1))
    arrived(("token", 1))
    greet(2, y_peer)
    chunk = 256
    part = chunk // 2
    per = chunk // (4 * rows)
    ro, co = iota((chunk, 1), 0), iota((1, chunk), 1)
    far_o = lax.rem(lax.rem(ro // rows, 2) + core, 2)
    want = ((lax.rem(ro // (2 * rows), per) * 2 + far_o) * 2 + ro // part) * rows + lax.rem(ro, rows)
    sort_in[...] = one_hot(want, co)
    chip_o = ro // (4 * rows)
    t_o = lax.rem(ro // rows, 2)
    want = ((t_o * per + chip_o) * 2 + core) * rows + lax.rem(ro, rows)
    far_o = lax.rem(ro // (2 * rows), 2)
    sort_own[...] = one_hot(jnp.where(far_o == 0, want, -1), co)
    sort_sib[...] = one_hot(jnp.where(far_o == 1, want, -1), co)
    arrived(("token", 2))
    greet(3, y_peer)
    for i in range(1, len(loads)):
        arrived(("load", i))
    arrived(("token", 3))
    greet(4, y_peer)

    arrived("groups sent")
    for t in range(2):
        for d in (1, -1):
            mine = r_full.at[t, column(x), :]
            remote(mine, mine, r_send, r_near, (x_peer(d), f)).start()
    for t in range(2):
        for d in (1, -1):
            mine = l_full.at[t, :, column(x)]
            remote(mine, mine, l_send, l_near, (x_peer(d), f)).start()
    near_rows = pl.ds(0, 2 * quarter)
    started("right near", r_full.at[:, near_rows, :], r_near)
    started("right sent", r_full.at[:, near_rows, :], r_send)
    started("left near", l_full.at[:, near_rows, :], l_near)
    started("left sent", l_full.at[:, near_rows, :], l_send)

    arrived("groups")
    total = raw[0].astype(F32) + raw[1].astype(F32) + raw[2].astype(F32) + raw[3].astype(F32)
    mean[0] = (total * (1.0 / groups)).astype(BF16).reshape(many, LANES)
    share = remote(mean.at[0], mean.at[1], x_send, x_recv, sibling)
    share.start()
    pending["mean"] = share.wait
    near = dot(pick[...], mean[0]).reshape(chips, 2 * rows, LANES)
    arrived("mean")
    away = dot(pick[...], mean[1]).reshape(chips, 2 * rows, LANES)
    send_b[...] = jnp.concatenate([near, away], axis=1).astype(BF16)

    arrived(("token", 4))

    along_z = [lax.rem(z + d, LINE) for d in range(LINE)]
    along_y = [lax.rem(y + d, LINE) for d in range(LINE)]

    def all_to_all(name, src, dst, send, recv):
        for dz, dy in far_first:
            to = along_z[dz] * LINE + along_y[dy]
            remote(src.at[to], dst.at[chip], send, recv, (x, to * 2 + core)).start()
        dst[chip] = src[chip]
        started(name, dst.at[pl.ds(0, chips - 1)], recv)
        started(name + " sent", src.at[pl.ds(0, chips - 1)], send)

    all_to_all("rows", send_b, recv_b, b_send, b_recv)

    arrived("right near")
    for t in range(2):
        for i, d in enumerate((1, -1)):
            piece = r_full.at[t, row_half(x_peer(-d), quarter, i), :]
            remote(piece, piece, r_send, r_far, (x_peer(d), f)).start()
    started("right", r_full.at[:, pl.ds(0, quarter), :], r_far)
    started("right sent", r_full.at[:, parts, :], r_send)

    arrived("rows")
    for j in range(chips // per):
        rows_j = dot(sort_in[...], recv_b[j * per : (j + 1) * per].reshape(chunk, LANES)).astype(BF16)
        for t in range(2):
            g_full[t, j * part : (j + 1) * part, column(x)] = rows_j[t * part : (t + 1) * part]
    for t in range(2):
        for d in (1, -1):
            mine = g_full.at[t, :, column(x)]
            remote(mine, mine, c_send, c_near.at[t], (x_peer(d), f)).start()
        started(("block near", t), g_full.at[t, pl.ds(0, 2 * quarter), :], c_near.at[t])
    started("blocks sent", g_full.at[:, pl.ds(0, 2 * quarter), :], c_send)
    for t in range(2):
        arrived(("block near", t))
        for i, d in enumerate((1, -1)):
            piece = g_full.at[t, pl.ds(i * (order // 2), order // 2), column(x_peer(-d))]
            remote(piece, piece, c_send, c_far.at[t], (x_peer(d), f)).start()
        started(("block", t), g_full.at[t, pl.ds(0, quarter), :], c_far.at[t])
    started("blocks sent", g_full.at[:, parts, :], c_send)
    arrived("left near")
    for t in range(2):
        for i, d in enumerate((1, -1)):
            piece = l_full.at[t, pl.ds(i * (order // 2), order // 2), column(x_peer(-d))]
            remote(piece, piece, l_send, l_far, (x_peer(d), f)).start()
    started("left", l_full.at[:, pl.ds(0, quarter), :], l_far)
    started("left sent", l_full.at[:, parts, :], l_send)
    arrived("right")

    def block_step(t):
        block = g_full[t]
        right = r_full[t]
        half_turn = dot(l_own[t], block, 0, 0).astype(BF16)
        rotated = dot(half_turn, right)
        moment = 0.95 * stat_m[t] + 0.05 * rotated * rotated
        new_moment_ref[t] = jnp.where(used[t] > 0.0, moment, stat_m[t])
        scaled = (rotated / (jnp.sqrt(moment) + epsilon)).astype(BF16)
        back_own[t] = dot(scaled, right, 1, 1).astype(BF16)
        for d in (2, 1, -1):
            p = x_peer(d)
            remote(
                back_own.at[t, :, column(p)], back_full.at[t, column(x), :],
                d_send, d_recv.at[t], (p, f),
            ).start()
        started(("back", t), back_full.at[t, parts, :], d_recv.at[t])
        started("back sent", back_full.at[pl.ds(0, t + 1), parts, :], d_send)
        back_full[t, column(x), :] = back_own[t, :, column(x)]

    def out_step(t):
        arrived(("back", t))
        out_own[t] = dot(l_full[t], back_full[t]).astype(BF16)
        remote(out_own.at[t], out_sib.at[t], y_send, y_recv.at[t], sibling).start()
        started(("out", t), out_sib.at[t], y_recv.at[t])
        started("out sent", out_own.at[pl.ds(0, t + 1)], y_send)

    arrived(("block", 0))
    block_step(0)
    arrived(("block", 1))
    block_step(1)
    arrived("left")
    out_step(0)
    out_step(1)
    def sort_rows(ref, sort, j):
        both = jnp.concatenate([ref[t, j * part : (j + 1) * part] for t in range(2)], axis=0)
        return dot(sort[...], both)

    mine = [sort_rows(out_own, sort_own, j) for j in range(chips // per)]
    arrived(("out", 0))
    arrived(("out", 1))
    for j in range(chips // per):
        both = (mine[j] + sort_rows(out_sib, sort_sib, j)).astype(BF16)
        send_e[j * per : (j + 1) * per] = both.reshape(per, 4 * rows, LANES)

    all_to_all("update", send_e, recv_e, e_send, e_recv)
    for t in range(2):
        block = g_full[t]
        left_term = dot(g_full[t, column(x), :], block, 1, 1)
        new_left_ref[t] = jnp.where(used[t] > 0.0, 0.95 * stat_l[t] + 0.05 * left_term, stat_l[t])
        right_term = dot(g_full[t, :, column(x)], block, 0, 0)
        new_right_ref[t] = jnp.where(used[t] > 0.0, 0.95 * stat_r[t] + 0.05 * right_term, stat_r[t])
    arrived("update")
    picked = dot(place[...], recv_e[...].reshape(chips * 4 * rows, LANES))
    update_ref[...] = picked.astype(BF16).reshape(layers, rows, blocks_per, LANES)
    finish()


def stay(array):
    return pltpu.with_memory_space_constraint(array, pltpu.HBM)


def store_kernel(*refs):
    count = (len(refs) - 1) // 2
    copies = [
        pltpu.make_async_copy(refs[i], refs[count + i], refs[-1].at[i]) for i in range(count)
    ]
    for copy in copies:
        copy.start()
    for copy in copies:
        copy.wait()


def local(gradient, owner_slot, stat_left, stat_right, second_moment, basis_left, basis_right):
    layers, row_dev, columns = gradient.shape[1:]
    capacity, quarter, order = basis_right.shape
    blocks_per = columns // order
    chips = LINE * LINE
    many = layers * blocks_per * row_dev
    pieces = gradient.reshape(layers, row_dev, blocks_per, order)
    vmem = pl.BlockSpec(memory_space=pltpu.VMEM)
    hbm = pl.BlockSpec(memory_space=pltpu.HBM)
    dma = pltpu.SemaphoreType.DMA
    message = (chips, 4 * row_dev, quarter)
    stat = (capacity, quarter, order)
    full = (capacity, order, order)
    results = pl.pallas_call(
        kernel,
        name="soap_step",
        out_shape=(
            pltpu.VMEM((layers, row_dev, blocks_per, quarter), BF16),
            pltpu.VMEM(stat, F32),
            pltpu.VMEM(stat, F32),
            pltpu.VMEM(stat, F32),
        ),
        in_specs=[hbm, pl.BlockSpec(memory_space=pl.ANY)] + [hbm] * 5,
        out_specs=[vmem] * 4,
        scratch_shapes=[
            pltpu.VMEM(owner_slot.shape, I32),
            pltpu.VMEM((4, layers, row_dev, blocks_per, quarter), BF16),
            pltpu.VMEM((2, many, quarter), BF16),
            pltpu.VMEM((chips * 2 * row_dev, many), BF16),
            pltpu.VMEM((many, chips * 4 * row_dev), BF16),
            pltpu.VMEM((256, 256), BF16),
            pltpu.VMEM((256, 256), BF16),
            pltpu.VMEM((256, 256), BF16),
            pltpu.VMEM(message, BF16),
            pltpu.VMEM(message, BF16),
            pltpu.VMEM(full, BF16),
            pltpu.VMEM(full, BF16),
            pltpu.VMEM(full, BF16),
            pltpu.VMEM((capacity, order, quarter), BF16),
            pltpu.VMEM((capacity, quarter, order), BF16),
            pltpu.VMEM((capacity, order, quarter), BF16),
            pltpu.VMEM((capacity, order, quarter), BF16),
            pltpu.VMEM((capacity, order, quarter), BF16),
            pltpu.VMEM(message, BF16),
            pltpu.VMEM(message, BF16),
            pltpu.VMEM(stat, F32),
            pltpu.VMEM(stat, F32),
            pltpu.VMEM(stat, F32),
            dma((10,)),
            dma, dma,
            dma, dma,
            dma, dma,
            dma, dma((2,)), dma((2,)),
            dma, dma, dma,
            dma, dma, dma,
            dma, dma((2,)),
            dma, dma((2,)),
            dma, dma,
            pltpu.SemaphoreType.REGULAR((5,)),
        ],
        compiler_params=pltpu.CompilerParams(
            collective_id=0, has_side_effects=True, vmem_limit_bytes=40 << 20
        ),
    )(stay(owner_slot), pieces, *(stay(a) for a in (stat_left, stat_right, second_moment, basis_left, basis_right)))
    return pl.pallas_call(
        store_kernel,
        name="store",
        out_shape=tuple(jax.ShapeDtypeStruct(r.shape, r.dtype) for r in results),
        in_specs=[vmem] * 4,
        out_specs=[hbm] * 4,
        scratch_shapes=[dma((4,))],
        compiler_params=pltpu.CompilerParams(vmem_limit_bytes=8 << 20),
    )(*results)


def solution(mesh):
    placed = (
        P("dp", None, "fsdp", None),
        P(),
        P("fsdp", "dp", None),
        P("fsdp", "dp", None),
        P("fsdp", "dp", None),
        P("fsdp", None, "dp"),
        P("fsdp", "dp", None),
    )
    return jax.shard_map(
        local,
        mesh=mesh,
        in_specs=placed,
        out_specs=(
            P(None, "fsdp", None, "dp"),
            P("fsdp", "dp", None),
            P("fsdp", "dp", None),
            P("fsdp", "dp", None),
        ),
        check_vma=False,
    )
```

```python
import functools

import jax
import jax.numpy as jnp
from jax import lax
from jax.experimental import pallas as pl
from jax.experimental.pallas import tpu as pltpu
from jax.sharding import PartitionSpec as P

epsilon = 1e-08
MESH = pl.DeviceIdType.MESH
F32, BF16, I32 = jnp.float32, jnp.bfloat16, jnp.int32
LINE = 8
LANES = 128


def hops(d):
    return min(d, LINE - d)


far_first = sorted(
    ((dz, dy) for dz in range(LINE) for dy in range(LINE) if dz or dy),
    key=lambda step: -hops(step[0]) - hops(step[1]),
)


def iota(shape, dim):
    return lax.broadcasted_iota(I32, shape, dim)


def dot(a, b, ca=1, cb=0):
    return lax.dot_general(a, b, (((ca,), (cb,)), ((), ())), preferred_element_type=F32)


def one_hot(rows, columns):
    return jnp.where(rows == columns, 1.0, 0.0).astype(BF16)


def kernel(
    slot_ref, grad_ref, left_ref, right_ref, moment_ref, bl_ref, br_ref,
    update_ref, new_left_ref, new_right_ref, new_moment_ref,
    slot_vmem, grad, parted, raw, mean, pick, place, sort_in, sort_own, sort_sib,
    send_b, recv_b, g_full, l_full, r_full, l_own, l_turned, rotated_ref, back_own, back_full,
    out_own, out_sib, send_e, recv_e, stat_l, stat_r, stat_m,
    local_sem, a_send, a_recv, x_send, x_recv, b_send, b_recv, c_send, c_near, c_far,
    l_send, l_near, l_far, r_send, r_near, r_far, d_send, d_recv, y_send, y_recv,
    e_send, e_recv, tokens,
):
    x = lax.axis_index("dp")
    f = lax.axis_index("fsdp")
    groups = 4
    core = lax.rem(f, 2)
    chip = f // 2
    z, y = chip // LINE, lax.rem(chip, LINE)
    chips = LINE * LINE
    sibling = (x, f + 1 - 2 * core)
    layers, rows, columns = grad_ref.shape
    order = g_full.shape[1]
    blocks_per = columns // order
    many = layers * rows * blocks_per
    quarter = order // groups
    half = quarter // 2
    parts = pl.ds(0, order - quarter)

    def x_peer(d):
        return lax.rem(x + d + groups, groups)

    def device(zz, yy):
        return (x, (zz * LINE + yy) * 2 + core)

    def z_peer(d):
        return device(lax.rem(z + d + LINE, LINE), y)

    def y_peer(d):
        return device(z, lax.rem(y + d + LINE, LINE))

    def column(p):
        return pl.ds(pl.multiple_of(p * LANES, LANES), LANES)

    def row_half(p, size, which):
        return pl.ds(pl.multiple_of(p * size + which * (size // 2), size // 2), size // 2)

    def remote(src, dst, send, recv, to):
        return pltpu.make_async_remote_copy(
            src_ref=src, dst_ref=dst, send_sem=send, recv_sem=recv,
            device_id=to, device_id_type=MESH,
        )

    def signal(sem, to):
        pl.semaphore_signal(sem, inc=1, device_id=to, device_id_type=MESH)

    pending = {}

    def started(name, ref, sem):
        pending[name] = lambda: pltpu.make_async_copy(ref, ref, sem).wait()

    def arrived(name):
        pending.pop(name)()

    def finish():
        for name in list(pending):
            arrived(name)

    barrier = pltpu.get_barrier_semaphore()
    for d in (2, 1, -1):
        signal(barrier, (x_peer(d), f))
    for d in (1, -1):
        signal(barrier, z_peer(d))
        signal(barrier, y_peer(d))
    signal(barrier, sibling)

    loads = [
        pltpu.make_async_copy(slot_ref, slot_vmem, local_sem.at[0]),
        pltpu.make_async_copy(grad_ref, grad, local_sem.at[1]),
        pltpu.make_async_copy(bl_ref, l_own, local_sem.at[2]),
        pltpu.make_async_copy(left_ref, stat_l, local_sem.at[3]),
        pltpu.make_async_copy(right_ref, stat_r, local_sem.at[4]),
        pltpu.make_async_copy(moment_ref, stat_m, local_sem.at[5]),
    ]
    for t in range(2):
        loads.append(pltpu.make_async_copy(bl_ref.at[t], l_full.at[t, :, column(x)], local_sem.at[6 + t]))
        loads.append(pltpu.make_async_copy(br_ref.at[t], r_full.at[t, column(x), :], local_sem.at[8 + t]))
    loads[1].start()
    for i, load in enumerate(loads):
        if i != 1:
            load.start()
        pending["load", i] = load.wait
    def cut(at, d, h):
        p = x_peer(d)
        for l in range(h * some, (h + 1) * some):
            pieces = [
                grad[l, :, pl.ds(pl.multiple_of(c * order + p * LANES, LANES), LANES)].astype(F32)
                for c in range(blocks_per)
            ]
            size = rows * blocks_per
            parted[at, l * size : (l + 1) * size] = jnp.concatenate(pieces, axis=0).astype(BF16)

    some = layers // 2
    peers = ((1, 2), (0, 1), (2, -1))
    arrived(("load", 1))
    cut(*peers[0], 0)
    pl.semaphore_wait(barrier, 8)

    for h in range(2):
        held = pl.ds(h * (many // 2), many // 2)
        for at, d in peers:
            if (at, h) != (peers[0][0], 0):
                cut(at, d, h)
            remote(
                parted.at[at, held], raw.at[at, held], a_send, a_recv.at[h], (x_peer(d), f)
            ).start()
        started(("groups", h), raw.at[pl.ds(0, 3), held], a_recv.at[h])
    started("groups sent", raw.at[pl.ds(0, 3)], a_send)
    for h in range(2):
        cut(3, 0, h)

    def greet(i, peers):
        for d in (1, -1):
            signal(tokens.at[i], peers(d * (2 if i in (1, 4) else 1)))
        pending["token", i] = lambda: pl.semaphore_wait(tokens.at[i], 2)

    greet(0, z_peer)

    arrived(("load", 0))
    slots = slot_vmem[...].astype(F32).astype(BF16)
    spread = one_hot(lax.rem(iota((blocks_per, many), 1) // rows, blocks_per), iota((blocks_per, many), 0))
    wide = dot(slots, spread)
    own_layer = iota((layers, many), 1) // (rows * blocks_per) == iota((layers, many), 0)
    slot_lane = jnp.sum(jnp.where(own_layer, wide, 0.0), axis=0, keepdims=True).astype(I32)
    row_lane = lax.rem(iota((1, many), 1), rows)
    owner_lane = slot_lane // 2
    code_lane = jnp.where(
        lax.rem(owner_lane, 2) == core,
        (owner_lane // 2) * 2 * rows + lax.rem(slot_lane, 2) * rows + row_lane, -1,
    )
    used = [jnp.max(jnp.where(slot_lane == 2 * f + t, 1.0, 0.0), axis=1, keepdims=True) for t in range(2)]
    pick[...] = one_hot(code_lane, iota((chips * 2 * rows, many), 0))
    arrived(("token", 0))
    greet(1, z_peer)
    tall_spread = one_hot(lax.rem(iota((many, blocks_per), 0), blocks_per), iota((many, blocks_per), 1))
    tall = dot(tall_spread, slots, 1, 1)
    tall_layer = iota((many, layers), 0) // (rows * blocks_per) == iota((many, layers), 1)
    slot_col = jnp.sum(jnp.where(tall_layer, tall, 0.0), axis=1, keepdims=True).astype(I32)
    row_col = lax.rem(iota((many, 1), 0) // blocks_per, rows)
    owner_col = slot_col // 2
    far = jnp.where(lax.rem(owner_col, 2) == core, 0, 1)
    code_col = ((owner_col // 2) * 2 + far) * 2 * rows + lax.rem(slot_col, 2) * rows + row_col
    place[...] = one_hot(code_col, iota((many, chips * 4 * rows), 1))
    arrived(("token", 1))
    greet(2, y_peer)
    chunk = 256
    part = chunk // 2
    per = chunk // (4 * rows)
    ro, co = iota((chunk, 1), 0), iota((1, chunk), 1)
    far_o = lax.rem(lax.rem(ro // rows, 2) + core, 2)
    want = ((lax.rem(ro // (2 * rows), per) * 2 + far_o) * 2 + ro // part) * rows + lax.rem(ro, rows)
    sort_in[...] = one_hot(want, co)
    chip_o = ro // (4 * rows)
    t_o = lax.rem(ro // rows, 2)
    want = ((t_o * per + chip_o) * 2 + core) * rows + lax.rem(ro, rows)
    far_o = lax.rem(ro // (2 * rows), 2)
    sort_own[...] = one_hot(jnp.where(far_o == 0, want, -1), co)
    sort_sib[...] = one_hot(jnp.where(far_o == 1, want, -1), co)
    arrived(("token", 2))
    greet(3, y_peer)
    for i in range(2, len(loads)):
        arrived(("load", i))
    for t in range(2):
        l_turned[t] = l_own[t].astype(F32).T.astype(BF16)
    arrived(("token", 3))
    greet(4, y_peer)

    def add_groups(h):
        arrived(("groups", h))
        lines = pl.ds(h * (many // 2), many // 2)
        total = parted[3, lines].astype(F32)
        for g in range(groups - 1):
            total = total + raw[g, lines].astype(F32)
        mean[0, lines] = (total * (1.0 / groups)).astype(BF16)
        remote(mean.at[0, lines], mean.at[1, lines], x_send, x_recv.at[h], sibling).start()
        started(("mean", h), mean.at[1, lines], x_recv.at[h])
        started("mean sent", mean.at[0, pl.ds(0, (h + 1) * (many // 2))], x_send)

    add_groups(0)
    arrived("groups sent")
    for t in range(2):
        for d in (1, -1):
            mine = r_full.at[t, column(x), :]
            remote(mine, mine, r_send, r_near, (x_peer(d), f)).start()
    for t in range(2):
        for d in (1, -1):
            mine = l_full.at[t, :, column(x)]
            remote(mine, mine, l_send, l_near, (x_peer(d), f)).start()
    near_rows = pl.ds(0, 2 * quarter)
    started("right near", r_full.at[:, near_rows, :], r_near)
    started("right sent", r_full.at[:, near_rows, :], r_send)
    started("left near", l_full.at[:, near_rows, :], l_near)
    started("left sent", l_full.at[:, near_rows, :], l_send)

    add_groups(1)
    arrived(("mean", 0))
    arrived(("mean", 1))

    arrived(("token", 4))

    along_z = [lax.rem(z + d, LINE) for d in range(LINE)]
    along_y = [lax.rem(y + d, LINE) for d in range(LINE)]

    def all_to_all(name, fill, src, dst, send, recv):
        for k in range(LINE // 2):
            fill(k, lax.rem(z // 2 + k, LINE // 2))
        for dz, dy in far_first:
            to = along_z[dz] * LINE + along_y[dy]
            remote(src.at[to], dst.at[chip], send, recv, (x, to * 2 + core)).start()
        dst[chip] = src[chip]
        started(name, dst.at[pl.ds(0, chips - 1)], recv)
        started(name + " sent", src.at[pl.ds(0, chips - 1)], send)

    def fill_rows(k, j):
        lines = pl.ds(pl.multiple_of(j * part, part), part)
        near, away = (
            dot(pick[lines, :], mean[i]).reshape(per, 2 * rows, LANES) for i in range(2)
        )
        send_b[pl.ds(j * per, per)] = jnp.concatenate([near, away], axis=1).astype(BF16)

    all_to_all("rows", fill_rows, send_b, recv_b, b_send, b_recv)

    arrived("right near")
    for t in range(2):
        for i, d in enumerate((1, -1)):
            piece = r_full.at[t, row_half(x_peer(-d), quarter, i), :]
            remote(piece, piece, r_send, r_far, (x_peer(d), f)).start()
    started("right", r_full.at[:, pl.ds(0, quarter), :], r_far)
    started("right sent", r_full.at[:, parts, :], r_send)

    arrived("rows")
    for j in range(chips // per):
        rows_j = dot(sort_in[...], recv_b[j * per : (j + 1) * per].reshape(chunk, LANES)).astype(BF16)
        for t in range(2):
            g_full[t, j * part : (j + 1) * part, column(x)] = rows_j[t * part : (t + 1) * part]
    for t in range(2):
        for d in (1, -1):
            mine = g_full.at[t, :, column(x)]
            remote(mine, mine, c_send, c_near.at[t], (x_peer(d), f)).start()
        started(("block near", t), g_full.at[t, pl.ds(0, 2 * quarter), :], c_near.at[t])
    started("blocks sent", g_full.at[:, pl.ds(0, 2 * quarter), :], c_send)
    for t in range(2):
        arrived(("block near", t))
        for i, d in enumerate((1, -1)):
            piece = g_full.at[t, pl.ds(i * (order // 2), order // 2), column(x_peer(-d))]
            remote(piece, piece, c_send, c_far.at[t], (x_peer(d), f)).start()
        started(("block", t), g_full.at[t, pl.ds(0, quarter), :], c_far.at[t])
    started("blocks sent", g_full.at[:, parts, :], c_send)
    arrived("left near")
    for t in range(2):
        for i, d in enumerate((1, -1)):
            piece = l_full.at[t, pl.ds(i * (order // 2), order // 2), column(x_peer(-d))]
            remote(piece, piece, l_send, l_far, (x_peer(d), f)).start()
    started("left", l_full.at[:, pl.ds(0, quarter), :], l_far)
    started("left sent", l_full.at[:, parts, :], l_send)
    arrived("right")

    def turn(t, pieces):
        total = 0.0
        for p in pieces:
            half_turn = dot(l_turned[t], g_full[t, :, column(p)]).astype(BF16)
            total = total + dot(half_turn, r_full[t, column(p), :])
        return total

    for t in range(2):
        rotated_ref[t] = turn(t, (x, x_peer(1), x_peer(-1)))

    def block_step(t):
        rotated = rotated_ref[t] + turn(t, (x_peer(2),))
        right = r_full[t]
        moment = 0.95 * stat_m[t] + 0.05 * rotated * rotated
        new_moment_ref[t] = jnp.where(used[t] > 0.0, moment, stat_m[t])
        scaled = (rotated / (jnp.sqrt(moment) + epsilon)).astype(BF16)
        back_own[t] = dot(scaled, right, 1, 1).astype(BF16)
        for d in (2, 1, -1):
            p = x_peer(d)
            remote(
                back_own.at[t, :, column(p)], back_full.at[t, column(x), :],
                d_send, d_recv.at[t], (p, f),
            ).start()
        started(("back", t), back_full.at[t, parts, :], d_recv.at[t])
        started("back sent", back_full.at[pl.ds(0, t + 1), parts, :], d_send)
        back_full[t, column(x), :] = back_own[t, :, column(x)]

    def out_step(t):
        arrived(("back", t))
        out_own[t] = dot(l_full[t], back_full[t]).astype(BF16)
        remote(out_own.at[t], out_sib.at[t], y_send, y_recv.at[t], sibling).start()
        started(("out", t), out_sib.at[t], y_recv.at[t])
        started("out sent", out_own.at[pl.ds(0, t + 1)], y_send)

    arrived(("block", 0))
    block_step(0)
    arrived(("block", 1))
    block_step(1)
    arrived("left")
    out_step(0)
    out_step(1)
    def sort_rows(ref, sort, j):
        lines = pl.ds(pl.multiple_of(j * part, part), part)
        both = jnp.concatenate([ref[t, lines, :] for t in range(2)], axis=0)
        return dot(sort[...], both)

    mine = [sort_rows(out_own, sort_own, lax.rem(z // 2 + k, LINE // 2)) for k in range(LINE // 2)]
    arrived(("out", 0))
    arrived(("out", 1))

    def fill_update(k, j):
        both = (mine[k] + sort_rows(out_sib, sort_sib, j)).astype(BF16)
        send_e[pl.ds(j * per, per)] = both.reshape(per, 4 * rows, LANES)

    all_to_all("update", fill_update, send_e, recv_e, e_send, e_recv)
    for t in range(2):
        block = g_full[t]
        left_term = dot(g_full[t, column(x), :], block, 1, 1)
        new_left_ref[t] = jnp.where(used[t] > 0.0, 0.95 * stat_l[t] + 0.05 * left_term, stat_l[t])
        right_term = dot(g_full[t, :, column(x)], block, 0, 0)
        new_right_ref[t] = jnp.where(used[t] > 0.0, 0.95 * stat_r[t] + 0.05 * right_term, stat_r[t])
    arrived("update")
    picked = dot(place[...], recv_e[...].reshape(chips * 4 * rows, LANES))
    update_ref[...] = picked.astype(BF16).reshape(layers, rows, blocks_per, LANES)
    finish()


def stay(array):
    return pltpu.with_memory_space_constraint(array, pltpu.HBM)


def store_kernel(*refs):
    count = (len(refs) - 1) // 2
    copies = [
        pltpu.make_async_copy(refs[i], refs[count + i], refs[-1].at[i]) for i in range(count)
    ]
    for copy in copies:
        copy.start()
    for copy in copies:
        copy.wait()


def local(gradient, owner_slot, stat_left, stat_right, second_moment, basis_left, basis_right):
    layers, row_dev, columns = gradient.shape[1:]
    capacity, quarter, order = basis_right.shape
    blocks_per = columns // order
    chips = LINE * LINE
    many = layers * blocks_per * row_dev
    vmem = pl.BlockSpec(memory_space=pltpu.VMEM)
    hbm = pl.BlockSpec(memory_space=pltpu.HBM)
    dma = pltpu.SemaphoreType.DMA
    message = (chips, 4 * row_dev, quarter)
    stat = (capacity, quarter, order)
    full = (capacity, order, order)
    results = pl.pallas_call(
        kernel,
        name="soap_step",
        out_shape=(
            pltpu.VMEM((layers, row_dev, blocks_per, quarter), BF16),
            pltpu.VMEM(stat, F32),
            pltpu.VMEM(stat, F32),
            pltpu.VMEM(stat, F32),
        ),
        in_specs=[hbm] * 7,
        out_specs=[vmem] * 4,
        scratch_shapes=[
            pltpu.VMEM(owner_slot.shape, I32),
            pltpu.VMEM(gradient.shape[1:], BF16),
            pltpu.VMEM((4, many, quarter), BF16),
            pltpu.VMEM((3, many, quarter), BF16),
            pltpu.VMEM((2, many, quarter), BF16),
            pltpu.VMEM((chips * 2 * row_dev, many), BF16),
            pltpu.VMEM((many, chips * 4 * row_dev), BF16),
            pltpu.VMEM((256, 256), BF16),
            pltpu.VMEM((256, 256), BF16),
            pltpu.VMEM((256, 256), BF16),
            pltpu.VMEM(message, BF16),
            pltpu.VMEM(message, BF16),
            pltpu.VMEM(full, BF16),
            pltpu.VMEM(full, BF16),
            pltpu.VMEM(full, BF16),
            pltpu.VMEM((capacity, order, quarter), BF16),
            pltpu.VMEM((capacity, quarter, order), BF16),
            pltpu.VMEM(stat, F32),
            pltpu.VMEM((capacity, quarter, order), BF16),
            pltpu.VMEM((capacity, order, quarter), BF16),
            pltpu.VMEM((capacity, order, quarter), BF16),
            pltpu.VMEM((capacity, order, quarter), BF16),
            pltpu.VMEM(message, BF16),
            pltpu.VMEM(message, BF16),
            pltpu.VMEM(stat, F32),
            pltpu.VMEM(stat, F32),
            pltpu.VMEM(stat, F32),
            dma((10,)),
            dma, dma((2,)),
            dma, dma((2,)),
            dma, dma,
            dma, dma((2,)), dma((2,)),
            dma, dma, dma,
            dma, dma, dma,
            dma, dma((2,)),
            dma, dma((2,)),
            dma, dma,
            pltpu.SemaphoreType.REGULAR((5,)),
        ],
        compiler_params=pltpu.CompilerParams(
            collective_id=0, has_side_effects=True, vmem_limit_bytes=40 << 20
        ),
    )(*(stay(a) for a in (owner_slot, gradient[0], stat_left, stat_right, second_moment, basis_left, basis_right)))
    return pl.pallas_call(
        store_kernel,
        name="store",
        out_shape=tuple(jax.ShapeDtypeStruct(r.shape, r.dtype) for r in results),
        in_specs=[vmem] * 4,
        out_specs=[hbm] * 4,
        scratch_shapes=[dma((4,))],
        compiler_params=pltpu.CompilerParams(vmem_limit_bytes=8 << 20),
    )(*results)


def solution(mesh):
    placed = (
        P("dp", None, "fsdp", None),
        P(),
        P("fsdp", "dp", None),
        P("fsdp", "dp", None),
        P("fsdp", "dp", None),
        P("fsdp", None, "dp"),
        P("fsdp", "dp", None),
    )
    return jax.shard_map(
        local,
        mesh=mesh,
        in_specs=placed,
        out_specs=(
            P(None, "fsdp", None, "dp"),
            P("fsdp", "dp", None),
            P("fsdp", "dp", None),
            P("fsdp", "dp", None),
        ),
        check_vma=False,
    )
```

```python
import functools

import jax
import jax.numpy as jnp
from jax import lax
from jax.experimental import pallas as pl
from jax.experimental.pallas import tpu as pltpu
from jax.sharding import PartitionSpec as P

epsilon = 1e-08
MESH = pl.DeviceIdType.MESH
F32, BF16, I32 = jnp.float32, jnp.bfloat16, jnp.int32
LINE = 8
LANES = 128


def hops(d):
    return min(d, LINE - d)


far_first = sorted(
    ((dz, dy) for dz in range(LINE) for dy in range(LINE) if dz or dy),
    key=lambda step: -hops(step[0]) - hops(step[1]),
)


def iota(shape, dim):
    return lax.broadcasted_iota(I32, shape, dim)


def dot(a, b, ca=1, cb=0):
    return lax.dot_general(a, b, (((ca,), (cb,)), ((), ())), preferred_element_type=F32)


def one_hot(rows, columns):
    return jnp.where(rows == columns, 1.0, 0.0).astype(BF16)


def kernel(
    slot_ref, grad_ref, left_ref, right_ref, moment_ref, bl_ref, br_ref,
    update_ref, new_left_ref, new_right_ref, new_moment_ref,
    slot_vmem, grad, parted, raw, mean, pick, place, sort_in, sort_own, sort_sib,
    send_b, recv_b, g_full, l_full, r_full, l_own, l_turned, rotated_ref, back_own, back_full,
    out_own, out_sib, send_e, recv_e, stat_l, stat_r, stat_m,
    local_sem, a_send, a_recv, x_send, x_recv, b_send, b_recv, c_send, c_near, c_far,
    l_send, l_near, l_far, r_send, r_near, r_far, d_send, d_recv, y_send, y_recv,
    e_send, e_recv, tokens,
):
    x = lax.axis_index("dp")
    f = lax.axis_index("fsdp")
    groups = 4
    core = lax.rem(f, 2)
    chip = f // 2
    z, y = chip // LINE, lax.rem(chip, LINE)
    chips = LINE * LINE
    sibling = (x, f + 1 - 2 * core)
    layers, rows, columns = grad_ref.shape
    order = g_full.shape[1]
    blocks_per = columns // order
    many = layers * rows * blocks_per
    quarter = order // groups
    half = quarter // 2
    parts = pl.ds(0, order - quarter)

    def x_peer(d):
        return lax.rem(x + d + groups, groups)

    def device(zz, yy):
        return (x, (zz * LINE + yy) * 2 + core)

    def z_peer(d):
        return device(lax.rem(z + d + LINE, LINE), y)

    def y_peer(d):
        return device(z, lax.rem(y + d + LINE, LINE))

    def column(p):
        return pl.ds(pl.multiple_of(p * LANES, LANES), LANES)

    def row_half(p, size, which):
        return pl.ds(pl.multiple_of(p * size + which * (size // 2), size // 2), size // 2)

    def remote(src, dst, send, recv, to):
        return pltpu.make_async_remote_copy(
            src_ref=src, dst_ref=dst, send_sem=send, recv_sem=recv,
            device_id=to, device_id_type=MESH,
        )

    def signal(sem, to):
        pl.semaphore_signal(sem, inc=1, device_id=to, device_id_type=MESH)

    pending = {}

    def started(name, ref, sem):
        pending[name] = lambda: pltpu.make_async_copy(ref, ref, sem).wait()

    def arrived(name):
        pending.pop(name)()

    def finish():
        for name in list(pending):
            arrived(name)

    barrier = pltpu.get_barrier_semaphore()
    for d in (2, 1, -1):
        signal(barrier, (x_peer(d), f))
    for d in (1, -1):
        signal(barrier, z_peer(d))
        signal(barrier, y_peer(d))
    signal(barrier, sibling)

    loads = [
        pltpu.make_async_copy(slot_ref, slot_vmem, local_sem.at[0]),
        pltpu.make_async_copy(grad_ref, grad, local_sem.at[1]),
        pltpu.make_async_copy(bl_ref, l_own, local_sem.at[2]),
        pltpu.make_async_copy(left_ref, stat_l, local_sem.at[3]),
        pltpu.make_async_copy(right_ref, stat_r, local_sem.at[4]),
        pltpu.make_async_copy(moment_ref, stat_m, local_sem.at[5]),
    ]
    for t in range(2):
        loads.append(pltpu.make_async_copy(bl_ref.at[t], l_full.at[t, :, column(x)], local_sem.at[6 + t]))
        loads.append(pltpu.make_async_copy(br_ref.at[t], r_full.at[t, column(x), :], local_sem.at[8 + t]))
    loads[1].start()
    for i, load in enumerate(loads):
        if i != 1:
            load.start()
        pending["load", i] = load.wait
    def cut(at, d, h):
        p = x_peer(d)
        for l in range(h * some, (h + 1) * some):
            pieces = [
                grad[l, :, pl.ds(pl.multiple_of(c * order + p * LANES, LANES), LANES)].astype(F32)
                for c in range(blocks_per)
            ]
            size = rows * blocks_per
            parted[at, l * size : (l + 1) * size] = jnp.concatenate(pieces, axis=0).astype(BF16)

    some = layers // 2
    peers = ((1, 2), (0, 1), (2, -1))
    arrived(("load", 1))
    cut(*peers[0], 0)
    pl.semaphore_wait(barrier, 8)

    for h in range(2):
        held = pl.ds(h * (many // 2), many // 2)
        for at, d in peers:
            if (at, h) != (peers[0][0], 0):
                cut(at, d, h)
            remote(
                parted.at[at, held], raw.at[at, held], a_send, a_recv.at[h], (x_peer(d), f)
            ).start()
        started(("groups", h), raw.at[pl.ds(0, 3), held], a_recv.at[h])
    started("groups sent", raw.at[pl.ds(0, 3)], a_send)
    for h in range(2):
        cut(3, 0, h)

    for i in range(6, 10):
        arrived(("load", i))
    for t in range(2):
        for d in (1, -1):
            mine = r_full.at[t, column(x), :]
            remote(mine, mine, r_send, r_near, (x_peer(d), f)).start()
    near_rows = pl.ds(0, 2 * quarter)
    started("right near", r_full.at[:, near_rows, :], r_near)
    started("right sent", r_full.at[:, near_rows, :], r_send)

    def greet(i, peers):
        for d in (1, -1):
            signal(tokens.at[i], peers(d * (2 if i in (1, 4) else 1)))
        pending["token", i] = lambda: pl.semaphore_wait(tokens.at[i], 2)

    greet(0, z_peer)

    arrived(("load", 0))
    slots = slot_vmem[...].astype(F32).astype(BF16)
    spread = one_hot(lax.rem(iota((blocks_per, many), 1) // rows, blocks_per), iota((blocks_per, many), 0))
    wide = dot(slots, spread)
    own_layer = iota((layers, many), 1) // (rows * blocks_per) == iota((layers, many), 0)
    slot_lane = jnp.sum(jnp.where(own_layer, wide, 0.0), axis=0, keepdims=True).astype(I32)
    row_lane = lax.rem(iota((1, many), 1), rows)
    owner_lane = slot_lane // 2
    code_lane = jnp.where(
        lax.rem(owner_lane, 2) == core,
        (owner_lane // 2) * 2 * rows + lax.rem(slot_lane, 2) * rows + row_lane, -1,
    )
    used = [jnp.max(jnp.where(slot_lane == 2 * f + t, 1.0, 0.0), axis=1, keepdims=True) for t in range(2)]
    pick[...] = one_hot(code_lane, iota((chips * 2 * rows, many), 0))
    arrived(("token", 0))
    greet(1, z_peer)
    tall_spread = one_hot(lax.rem(iota((many, blocks_per), 0), blocks_per), iota((many, blocks_per), 1))
    tall = dot(tall_spread, slots, 1, 1)
    tall_layer = iota((many, layers), 0) // (rows * blocks_per) == iota((many, layers), 1)
    slot_col = jnp.sum(jnp.where(tall_layer, tall, 0.0), axis=1, keepdims=True).astype(I32)
    row_col = lax.rem(iota((many, 1), 0) // blocks_per, rows)
    owner_col = slot_col // 2
    far = jnp.where(lax.rem(owner_col, 2) == core, 0, 1)
    code_col = ((owner_col // 2) * 2 + far) * 2 * rows + lax.rem(slot_col, 2) * rows + row_col
    place[...] = one_hot(code_col, iota((many, chips * 4 * rows), 1))
    arrived(("token", 1))
    greet(2, y_peer)
    chunk = 256
    part = chunk // 2
    per = chunk // (4 * rows)
    ro, co = iota((chunk, 1), 0), iota((1, chunk), 1)
    far_o = lax.rem(lax.rem(ro // rows, 2) + core, 2)
    want = ((lax.rem(ro // (2 * rows), per) * 2 + far_o) * 2 + ro // part) * rows + lax.rem(ro, rows)
    sort_in[...] = one_hot(want, co)
    chip_o = ro // (4 * rows)
    t_o = lax.rem(ro // rows, 2)
    want = ((t_o * per + chip_o) * 2 + core) * rows + lax.rem(ro, rows)
    far_o = lax.rem(ro // (2 * rows), 2)
    sort_own[...] = one_hot(jnp.where(far_o == 0, want, -1), co)
    sort_sib[...] = one_hot(jnp.where(far_o == 1, want, -1), co)
    arrived(("token", 2))
    greet(3, y_peer)
    for i in range(2, 6):
        arrived(("load", i))
    for t in range(2):
        l_turned[t] = l_own[t].astype(F32).T.astype(BF16)
    arrived(("token", 3))
    greet(4, y_peer)

    def add_groups(h):
        arrived(("groups", h))
        lines = pl.ds(h * (many // 2), many // 2)
        total = parted[3, lines].astype(F32)
        for g in range(groups - 1):
            total = total + raw[g, lines].astype(F32)
        mean[0, lines] = (total * (1.0 / groups)).astype(BF16)
        remote(mean.at[0, lines], mean.at[1, lines], x_send, x_recv.at[h], sibling).start()
        started(("mean", h), mean.at[1, lines], x_recv.at[h])
        started("mean sent", mean.at[0, pl.ds(0, (h + 1) * (many // 2))], x_send)

    add_groups(0)
    arrived("groups sent")
    for t in range(2):
        for d in (1, -1):
            mine = l_full.at[t, :, column(x)]
            remote(mine, mine, l_send, l_near, (x_peer(d), f)).start()
    started("left near", l_full.at[:, near_rows, :], l_near)
    started("left sent", l_full.at[:, near_rows, :], l_send)

    add_groups(1)
    arrived(("mean", 0))
    arrived(("mean", 1))

    arrived(("token", 4))

    along_z = [lax.rem(z + d, LINE) for d in range(LINE)]
    along_y = [lax.rem(y + d, LINE) for d in range(LINE)]

    def all_to_all(name, fill, src, dst, send, recv):
        for k in range(LINE // 2):
            fill(k, lax.rem(z // 2 + k, LINE // 2))
        for dz, dy in far_first:
            to = along_z[dz] * LINE + along_y[dy]
            remote(src.at[to], dst.at[chip], send, recv, (x, to * 2 + core)).start()
        dst[chip] = src[chip]
        started(name, dst.at[pl.ds(0, chips - 1)], recv)
        started(name + " sent", src.at[pl.ds(0, chips - 1)], send)

    def fill_rows(k, j):
        lines = pl.ds(pl.multiple_of(j * part, part), part)
        near, away = (
            dot(pick[lines, :], mean[i]).reshape(per, 2 * rows, LANES) for i in range(2)
        )
        send_b[pl.ds(j * per, per)] = jnp.concatenate([near, away], axis=1).astype(BF16)

    all_to_all("rows", fill_rows, send_b, recv_b, b_send, b_recv)

    arrived("right near")
    for t in range(2):
        for i, d in enumerate((1, -1)):
            piece = r_full.at[t, row_half(x_peer(-d), quarter, i), :]
            remote(piece, piece, r_send, r_far, (x_peer(d), f)).start()
    started("right", r_full.at[:, pl.ds(0, quarter), :], r_far)
    started("right sent", r_full.at[:, parts, :], r_send)

    arrived("rows")
    for j in range(chips // per):
        rows_j = dot(sort_in[...], recv_b[j * per : (j + 1) * per].reshape(chunk, LANES)).astype(BF16)
        for t in range(2):
            g_full[t, j * part : (j + 1) * part, column(x)] = rows_j[t * part : (t + 1) * part]
    for t in range(2):
        for d in (1, -1):
            mine = g_full.at[t, :, column(x)]
            remote(mine, mine, c_send, c_near.at[t], (x_peer(d), f)).start()
        started(("block near", t), g_full.at[t, pl.ds(0, 2 * quarter), :], c_near.at[t])
    started("blocks sent", g_full.at[:, pl.ds(0, 2 * quarter), :], c_send)
    for t in range(2):
        arrived(("block near", t))
        for i, d in enumerate((1, -1)):
            piece = g_full.at[t, pl.ds(i * (order // 2), order // 2), column(x_peer(-d))]
            remote(piece, piece, c_send, c_far.at[t], (x_peer(d), f)).start()
        started(("block", t), g_full.at[t, pl.ds(0, quarter), :], c_far.at[t])
    started("blocks sent", g_full.at[:, parts, :], c_send)
    arrived("left near")
    for t in range(2):
        for i, d in enumerate((1, -1)):
            piece = l_full.at[t, pl.ds(i * (order // 2), order // 2), column(x_peer(-d))]
            remote(piece, piece, l_send, l_far, (x_peer(d), f)).start()
    started("left", l_full.at[:, pl.ds(0, quarter), :], l_far)
    started("left sent", l_full.at[:, parts, :], l_send)
    arrived("right")

    def turn(t, pieces):
        total = 0.0
        for p in pieces:
            half_turn = dot(l_turned[t], g_full[t, :, column(p)]).astype(BF16)
            total = total + dot(half_turn, r_full[t, column(p), :])
        return total

    for t in range(2):
        rotated_ref[t] = turn(t, (x, x_peer(1), x_peer(-1)))

    def block_step(t):
        rotated = rotated_ref[t] + turn(t, (x_peer(2),))
        right = r_full[t]
        moment = 0.95 * stat_m[t] + 0.05 * rotated * rotated
        new_moment_ref[t] = jnp.where(used[t] > 0.0, moment, stat_m[t])
        scaled = (rotated / (jnp.sqrt(moment) + epsilon)).astype(BF16)
        back_own[t] = dot(scaled, right, 1, 1).astype(BF16)
        for d in (2, 1, -1):
            p = x_peer(d)
            remote(
                back_own.at[t, :, column(p)], back_full.at[t, column(x), :],
                d_send, d_recv.at[t], (p, f),
            ).start()
        started(("back", t), back_full.at[t, parts, :], d_recv.at[t])
        started("back sent", back_full.at[pl.ds(0, t + 1), parts, :], d_send)
        back_full[t, column(x), :] = back_own[t, :, column(x)]

    def out_step(t):
        arrived(("back", t))
        out_own[t] = dot(l_full[t], back_full[t]).astype(BF16)
        remote(out_own.at[t], out_sib.at[t], y_send, y_recv.at[t], sibling).start()
        started(("out", t), out_sib.at[t], y_recv.at[t])
        started("out sent", out_own.at[pl.ds(0, t + 1)], y_send)

    arrived(("block", 0))
    block_step(0)
    arrived(("block", 1))
    block_step(1)
    arrived("left")
    out_step(0)
    out_step(1)
    def sort_rows(ref, sort, j):
        lines = pl.ds(pl.multiple_of(j * part, part), part)
        both = jnp.concatenate([ref[t, lines, :] for t in range(2)], axis=0)
        return dot(sort[...], both)

    mine = [sort_rows(out_own, sort_own, lax.rem(z // 2 + k, LINE // 2)) for k in range(LINE // 2)]
    arrived(("out", 0))
    arrived(("out", 1))

    def fill_update(k, j):
        both = (mine[k] + sort_rows(out_sib, sort_sib, j)).astype(BF16)
        send_e[pl.ds(j * per, per)] = both.reshape(per, 4 * rows, LANES)

    all_to_all("update", fill_update, send_e, recv_e, e_send, e_recv)
    for t in range(2):
        block = g_full[t]
        left_term = dot(g_full[t, column(x), :], block, 1, 1)
        new_left_ref[t] = jnp.where(used[t] > 0.0, 0.95 * stat_l[t] + 0.05 * left_term, stat_l[t])
        right_term = dot(g_full[t, :, column(x)], block, 0, 0)
        new_right_ref[t] = jnp.where(used[t] > 0.0, 0.95 * stat_r[t] + 0.05 * right_term, stat_r[t])
    arrived("update")
    picked = dot(place[...], recv_e[...].reshape(chips * 4 * rows, LANES))
    update_ref[...] = picked.astype(BF16).reshape(layers, rows, blocks_per, LANES)
    finish()


def stay(array):
    return pltpu.with_memory_space_constraint(array, pltpu.HBM)


def store_kernel(*refs):
    count = (len(refs) - 1) // 2
    copies = [
        pltpu.make_async_copy(refs[i], refs[count + i], refs[-1].at[i]) for i in range(count)
    ]
    for copy in copies:
        copy.start()
    for copy in copies:
        copy.wait()


def local(gradient, owner_slot, stat_left, stat_right, second_moment, basis_left, basis_right):
    layers, row_dev, columns = gradient.shape[1:]
    capacity, quarter, order = basis_right.shape
    blocks_per = columns // order
    chips = LINE * LINE
    many = layers * blocks_per * row_dev
    vmem = pl.BlockSpec(memory_space=pltpu.VMEM)
    hbm = pl.BlockSpec(memory_space=pltpu.HBM)
    dma = pltpu.SemaphoreType.DMA
    message = (chips, 4 * row_dev, quarter)
    stat = (capacity, quarter, order)
    full = (capacity, order, order)
    results = pl.pallas_call(
        kernel,
        name="soap_step",
        out_shape=(
            pltpu.VMEM((layers, row_dev, blocks_per, quarter), BF16),
            pltpu.VMEM(stat, F32),
            pltpu.VMEM(stat, F32),
            pltpu.VMEM(stat, F32),
        ),
        in_specs=[hbm] * 7,
        out_specs=[vmem] * 4,
        scratch_shapes=[
            pltpu.VMEM(owner_slot.shape, I32),
            pltpu.VMEM(gradient.shape[1:], BF16),
            pltpu.VMEM((4, many, quarter), BF16),
            pltpu.VMEM((3, many, quarter), BF16),
            pltpu.VMEM((2, many, quarter), BF16),
            pltpu.VMEM((chips * 2 * row_dev, many), BF16),
            pltpu.VMEM((many, chips * 4 * row_dev), BF16),
            pltpu.VMEM((256, 256), BF16),
            pltpu.VMEM((256, 256), BF16),
            pltpu.VMEM((256, 256), BF16),
            pltpu.VMEM(message, BF16),
            pltpu.VMEM(message, BF16),
            pltpu.VMEM(full, BF16),
            pltpu.VMEM(full, BF16),
            pltpu.VMEM(full, BF16),
            pltpu.VMEM((capacity, order, quarter), BF16),
            pltpu.VMEM((capacity, quarter, order), BF16),
            pltpu.VMEM(stat, F32),
            pltpu.VMEM((capacity, quarter, order), BF16),
            pltpu.VMEM((capacity, order, quarter), BF16),
            pltpu.VMEM((capacity, order, quarter), BF16),
            pltpu.VMEM((capacity, order, quarter), BF16),
            pltpu.VMEM(message, BF16),
            pltpu.VMEM(message, BF16),
            pltpu.VMEM(stat, F32),
            pltpu.VMEM(stat, F32),
            pltpu.VMEM(stat, F32),
            dma((10,)),
            dma, dma((2,)),
            dma, dma((2,)),
            dma, dma,
            dma, dma((2,)), dma((2,)),
            dma, dma, dma,
            dma, dma, dma,
            dma, dma((2,)),
            dma, dma((2,)),
            dma, dma,
            pltpu.SemaphoreType.REGULAR((5,)),
        ],
        compiler_params=pltpu.CompilerParams(
            collective_id=0, has_side_effects=True, vmem_limit_bytes=40 << 20
        ),
    )(*(stay(a) for a in (owner_slot, gradient[0], stat_left, stat_right, second_moment, basis_left, basis_right)))
    return pl.pallas_call(
        store_kernel,
        name="store",
        out_shape=tuple(jax.ShapeDtypeStruct(r.shape, r.dtype) for r in results),
        in_specs=[vmem] * 4,
        out_specs=[hbm] * 4,
        scratch_shapes=[dma((4,))],
        compiler_params=pltpu.CompilerParams(vmem_limit_bytes=8 << 20),
    )(*results)


def solution(mesh):
    placed = (
        P("dp", None, "fsdp", None),
        P(),
        P("fsdp", "dp", None),
        P("fsdp", "dp", None),
        P("fsdp", "dp", None),
        P("fsdp", None, "dp"),
        P("fsdp", "dp", None),
    )
    return jax.shard_map(
        local,
        mesh=mesh,
        in_specs=placed,
        out_specs=(
            P(None, "fsdp", None, "dp"),
            P("fsdp", "dp", None),
            P("fsdp", "dp", None),
            P("fsdp", "dp", None),
        ),
        check_vma=False,
    )
```

```python
import functools

import jax
import jax.numpy as jnp
from jax import lax
from jax.experimental import pallas as pl
from jax.experimental.pallas import tpu as pltpu
from jax.sharding import PartitionSpec as P

epsilon = 1e-08
MESH = pl.DeviceIdType.MESH
F32, BF16, I32 = jnp.float32, jnp.bfloat16, jnp.int32
LINE = 8
LANES = 128


def hops(d):
    return min(d, LINE - d)


far_first = sorted(
    ((dz, dy) for dz in range(LINE) for dy in range(LINE) if dz or dy),
    key=lambda step: -hops(step[0]) - hops(step[1]),
)


def iota(shape, dim):
    return lax.broadcasted_iota(I32, shape, dim)


def dot(a, b, ca=1, cb=0):
    return lax.dot_general(a, b, (((ca,), (cb,)), ((), ())), preferred_element_type=F32)


def one_hot(rows, columns):
    return jnp.where(rows == columns, 1.0, 0.0).astype(BF16)


def kernel(
    slot_ref, grad_ref, left_ref, right_ref, moment_ref, bl_ref, br_ref,
    update_ref, new_left_ref, new_right_ref, new_moment_ref,
    slot_vmem, grad, parted, raw, mean, pick, place, sort_in, sort_own, sort_sib,
    send_b, recv_b, g_full, l_full, r_full, l_own, l_turned, rotated_ref, back_own, back_full,
    out_own, out_sib, send_e, recv_e, stat_l, stat_r, stat_m,
    local_sem, a_send, a_recv, x_send, x_recv, b_send, b_recv, c_send, c_near, c_far,
    l_send, l_near, l_far, r_send, r_near, r_far, d_send, d_recv, y_send, y_recv,
    e_send, e_recv, tokens,
):
    x = lax.axis_index("dp")
    f = lax.axis_index("fsdp")
    groups = 4
    core = lax.rem(f, 2)
    chip = f // 2
    z, y = chip // LINE, lax.rem(chip, LINE)
    chips = LINE * LINE
    sibling = (x, f + 1 - 2 * core)
    layers, rows, columns = grad_ref.shape
    order = g_full.shape[1]
    blocks_per = columns // order
    many = layers * rows * blocks_per
    quarter = order // groups
    half = quarter // 2
    parts = pl.ds(0, order - quarter)

    def x_peer(d):
        return lax.rem(x + d + groups, groups)

    def device(zz, yy):
        return (x, (zz * LINE + yy) * 2 + core)

    def z_peer(d):
        return device(lax.rem(z + d + LINE, LINE), y)

    def y_peer(d):
        return device(z, lax.rem(y + d + LINE, LINE))

    def column(p):
        return pl.ds(pl.multiple_of(p * LANES, LANES), LANES)

    def row_half(p, size, which):
        return pl.ds(pl.multiple_of(p * size + which * (size // 2), size // 2), size // 2)

    def remote(src, dst, send, recv, to):
        return pltpu.make_async_remote_copy(
            src_ref=src, dst_ref=dst, send_sem=send, recv_sem=recv,
            device_id=to, device_id_type=MESH,
        )

    def signal(sem, to):
        pl.semaphore_signal(sem, inc=1, device_id=to, device_id_type=MESH)

    pending = {}

    def started(name, ref, sem):
        pending[name] = lambda: pltpu.make_async_copy(ref, ref, sem).wait()

    def arrived(name):
        pending.pop(name)()

    def finish():
        for name in list(pending):
            arrived(name)

    barrier = pltpu.get_barrier_semaphore()
    for d in (2, 1, -1):
        signal(barrier, (x_peer(d), f))
    for d in (1, -1):
        signal(barrier, z_peer(d))
        signal(barrier, y_peer(d))
    signal(barrier, sibling)

    loads = [
        pltpu.make_async_copy(slot_ref, slot_vmem, local_sem.at[0]),
        pltpu.make_async_copy(grad_ref, grad, local_sem.at[1]),
        pltpu.make_async_copy(bl_ref, l_own, local_sem.at[2]),
        pltpu.make_async_copy(left_ref, stat_l, local_sem.at[3]),
        pltpu.make_async_copy(right_ref, stat_r, local_sem.at[4]),
        pltpu.make_async_copy(moment_ref, stat_m, local_sem.at[5]),
    ]
    for t in range(2):
        loads.append(pltpu.make_async_copy(bl_ref.at[t], l_full.at[t, :, column(x)], local_sem.at[6 + t]))
        loads.append(pltpu.make_async_copy(br_ref.at[t], r_full.at[t, column(x), :], local_sem.at[8 + t]))
    loads[1].start()
    for i, load in enumerate(loads):
        if i != 1:
            load.start()
        pending["load", i] = load.wait
    def cut(at, d, h):
        p = x_peer(d)
        for l in range(h * some, (h + 1) * some):
            pieces = [
                grad[l, :, pl.ds(pl.multiple_of(c * order + p * LANES, LANES), LANES)].astype(F32)
                for c in range(blocks_per)
            ]
            size = rows * blocks_per
            parted[at, l * size : (l + 1) * size] = jnp.concatenate(pieces, axis=0).astype(BF16)

    some = layers // 2
    peers = ((1, 2), (0, 1), (2, -1))
    arrived(("load", 1))
    cut(*peers[0], 0)
    pl.semaphore_wait(barrier, 8)

    def greet(i, peers):
        for d in (1, -1):
            signal(tokens.at[i], peers(d * (2 if i in (1, 4) else 1)))
        pending["token", i] = lambda: pl.semaphore_wait(tokens.at[i], 2)

    greet(0, z_peer)

    for h in range(2):
        held = pl.ds(h * (many // 2), many // 2)
        for at, d in peers:
            if (at, h) != (peers[0][0], 0):
                cut(at, d, h)
            remote(
                parted.at[at, held], raw.at[at, held], a_send, a_recv.at[h], (x_peer(d), f)
            ).start()
        started(("groups", h), raw.at[pl.ds(0, 3), held], a_recv.at[h])
    started("groups sent", raw.at[pl.ds(0, 3)], a_send)
    for h in range(2):
        cut(3, 0, h)

    for i in range(6, 10):
        arrived(("load", i))
    for t in range(2):
        for d in (1, -1):
            mine = r_full.at[t, column(x), :]
            remote(mine, mine, r_send, r_near, (x_peer(d), f)).start()
    near_rows = pl.ds(0, 2 * quarter)
    started("right near", r_full.at[:, near_rows, :], r_near)
    started("right sent", r_full.at[:, near_rows, :], r_send)

    arrived(("load", 0))
    slots = slot_vmem[...].astype(F32).astype(BF16)
    spread = one_hot(lax.rem(iota((blocks_per, many), 1) // rows, blocks_per), iota((blocks_per, many), 0))
    wide = dot(slots, spread)
    own_layer = iota((layers, many), 1) // (rows * blocks_per) == iota((layers, many), 0)
    slot_lane = jnp.sum(jnp.where(own_layer, wide, 0.0), axis=0, keepdims=True).astype(I32)
    row_lane = lax.rem(iota((1, many), 1), rows)
    owner_lane = slot_lane // 2
    code_lane = jnp.where(
        lax.rem(owner_lane, 2) == core,
        (owner_lane // 2) * 2 * rows + lax.rem(slot_lane, 2) * rows + row_lane, -1,
    )
    used = [jnp.max(jnp.where(slot_lane == 2 * f + t, 1.0, 0.0), axis=1, keepdims=True) for t in range(2)]
    pick[...] = one_hot(code_lane, iota((chips * 2 * rows, many), 0))
    arrived(("token", 0))
    greet(1, z_peer)
    tall_spread = one_hot(lax.rem(iota((many, blocks_per), 0), blocks_per), iota((many, blocks_per), 1))
    tall = dot(tall_spread, slots, 1, 1)
    tall_layer = iota((many, layers), 0) // (rows * blocks_per) == iota((many, layers), 1)
    slot_col = jnp.sum(jnp.where(tall_layer, tall, 0.0), axis=1, keepdims=True).astype(I32)
    row_col = lax.rem(iota((many, 1), 0) // blocks_per, rows)
    owner_col = slot_col // 2
    far = jnp.where(lax.rem(owner_col, 2) == core, 0, 1)
    code_col = ((owner_col // 2) * 2 + far) * 2 * rows + lax.rem(slot_col, 2) * rows + row_col
    place[...] = one_hot(code_col, iota((many, chips * 4 * rows), 1))
    arrived(("token", 1))
    greet(2, y_peer)
    chunk = 256
    part = chunk // 2
    per = chunk // (4 * rows)
    ro, co = iota((chunk, 1), 0), iota((1, chunk), 1)
    far_o = lax.rem(lax.rem(ro // rows, 2) + core, 2)
    want = ((lax.rem(ro // (2 * rows), per) * 2 + far_o) * 2 + ro // part) * rows + lax.rem(ro, rows)
    sort_in[...] = one_hot(want, co)
    chip_o = ro // (4 * rows)
    t_o = lax.rem(ro // rows, 2)
    want = ((t_o * per + chip_o) * 2 + core) * rows + lax.rem(ro, rows)
    far_o = lax.rem(ro // (2 * rows), 2)
    sort_own[...] = one_hot(jnp.where(far_o == 0, want, -1), co)
    sort_sib[...] = one_hot(jnp.where(far_o == 1, want, -1), co)
    arrived(("token", 2))
    greet(3, y_peer)
    for i in range(2, 6):
        arrived(("load", i))
    for t in range(2):
        l_turned[t] = l_own[t].astype(F32).T.astype(BF16)

    def add_groups(h):
        arrived(("groups", h))
        lines = pl.ds(h * (many // 2), many // 2)
        total = parted[3, lines].astype(F32)
        for g in range(groups - 1):
            total = total + raw[g, lines].astype(F32)
        mean[0, lines] = (total * (1.0 / groups)).astype(BF16)
        remote(mean.at[0, lines], mean.at[1, lines], x_send, x_recv.at[h], sibling).start()
        started(("mean", h), mean.at[1, lines], x_recv.at[h])
        started("mean sent", mean.at[0, pl.ds(0, (h + 1) * (many // 2))], x_send)

    add_groups(0)
    arrived(("token", 3))
    greet(4, y_peer)
    arrived("groups sent")
    for t in range(2):
        for d in (1, -1):
            mine = l_full.at[t, :, column(x)]
            remote(mine, mine, l_send, l_near, (x_peer(d), f)).start()
    started("left near", l_full.at[:, near_rows, :], l_near)
    started("left sent", l_full.at[:, near_rows, :], l_send)

    add_groups(1)
    near = [dot(pick[j * part : (j + 1) * part], mean[0]) for j in range(LINE // 2)]
    arrived(("mean", 0))
    arrived(("mean", 1))

    arrived(("token", 4))

    along_z = [lax.rem(z + d, LINE) for d in range(LINE)]
    along_y = [lax.rem(y + d, LINE) for d in range(LINE)]

    def all_to_all(name, fill, src, dst, send, recv):
        for j in range(LINE // 2):
            fill(j)
        for dz, dy in far_first:
            to = along_z[dz] * LINE + along_y[dy]
            remote(src.at[to], dst.at[chip], send, recv, (x, to * 2 + core)).start()
        dst[chip] = src[chip]
        started(name, dst.at[pl.ds(0, chips - 1)], recv)
        started(name + " sent", src.at[pl.ds(0, chips - 1)], send)

    def fill_rows(j):
        away = dot(pick[j * part : (j + 1) * part], mean[1])
        both = [v.reshape(per, 2 * rows, LANES) for v in (near[j], away)]
        send_b[j * per : (j + 1) * per] = jnp.concatenate(both, axis=1).astype(BF16)

    all_to_all("rows", fill_rows, send_b, recv_b, b_send, b_recv)

    arrived("right near")
    for t in range(2):
        for i, d in enumerate((1, -1)):
            piece = r_full.at[t, row_half(x_peer(-d), quarter, i), :]
            remote(piece, piece, r_send, r_far, (x_peer(d), f)).start()
    started("right", r_full.at[:, pl.ds(0, quarter), :], r_far)
    started("right sent", r_full.at[:, parts, :], r_send)

    arrived("rows")
    for j in range(chips // per):
        rows_j = dot(sort_in[...], recv_b[j * per : (j + 1) * per].reshape(chunk, LANES)).astype(BF16)
        for t in range(2):
            g_full[t, j * part : (j + 1) * part, column(x)] = rows_j[t * part : (t + 1) * part]
    for t in range(2):
        for d in (1, -1):
            mine = g_full.at[t, :, column(x)]
            remote(mine, mine, c_send, c_near.at[t], (x_peer(d), f)).start()
        started(("block near", t), g_full.at[t, pl.ds(0, 2 * quarter), :], c_near.at[t])
    started("blocks sent", g_full.at[:, pl.ds(0, 2 * quarter), :], c_send)
    for t in range(2):
        arrived(("block near", t))
        for i, d in enumerate((1, -1)):
            piece = g_full.at[t, pl.ds(i * (order // 2), order // 2), column(x_peer(-d))]
            remote(piece, piece, c_send, c_far.at[t], (x_peer(d), f)).start()
        started(("block", t), g_full.at[t, pl.ds(0, quarter), :], c_far.at[t])
    started("blocks sent", g_full.at[:, parts, :], c_send)
    arrived("left near")
    for t in range(2):
        for i, d in enumerate((1, -1)):
            piece = l_full.at[t, pl.ds(i * (order // 2), order // 2), column(x_peer(-d))]
            remote(piece, piece, l_send, l_far, (x_peer(d), f)).start()
    started("left", l_full.at[:, pl.ds(0, quarter), :], l_far)
    started("left sent", l_full.at[:, parts, :], l_send)
    arrived("right")

    def turn(t, pieces):
        total = 0.0
        for p in pieces:
            half_turn = dot(l_turned[t], g_full[t, :, column(p)]).astype(BF16)
            total = total + dot(half_turn, r_full[t, column(p), :])
        return total

    for t in range(2):
        rotated_ref[t] = turn(t, (x, x_peer(1), x_peer(-1)))

    def block_step(t):
        rotated = rotated_ref[t] + turn(t, (x_peer(2),))
        right = r_full[t]
        moment = 0.95 * stat_m[t] + 0.05 * rotated * rotated
        new_moment_ref[t] = jnp.where(used[t] > 0.0, moment, stat_m[t])
        scaled = (rotated / (jnp.sqrt(moment) + epsilon)).astype(BF16)
        back_own[t] = dot(scaled, right, 1, 1).astype(BF16)
        for d in (2, 1, -1):
            p = x_peer(d)
            remote(
                back_own.at[t, :, column(p)], back_full.at[t, column(x), :],
                d_send, d_recv.at[t], (p, f),
            ).start()
        started(("back", t), back_full.at[t, parts, :], d_recv.at[t])
        started("back sent", back_full.at[pl.ds(0, t + 1), parts, :], d_send)
        back_full[t, column(x), :] = back_own[t, :, column(x)]

    def out_step(t):
        arrived(("back", t))
        out_own[t] = dot(l_full[t], back_full[t]).astype(BF16)
        remote(out_own.at[t], out_sib.at[t], y_send, y_recv.at[t], sibling).start()
        started(("out", t), out_sib.at[t], y_recv.at[t])
        started("out sent", out_own.at[pl.ds(0, t + 1)], y_send)

    arrived(("block", 0))
    block_step(0)
    arrived(("block", 1))
    block_step(1)
    arrived("left")
    out_step(0)
    out_step(1)
    def sort_rows(ref, sort, j):
        both = jnp.concatenate([ref[t, j * part : (j + 1) * part] for t in range(2)], axis=0)
        return dot(sort[...], both)

    mine = [sort_rows(out_own, sort_own, j) for j in range(LINE // 2)]
    arrived(("out", 0))
    arrived(("out", 1))

    def fill_update(j):
        both = (mine[j] + sort_rows(out_sib, sort_sib, j)).astype(BF16)
        send_e[j * per : (j + 1) * per] = both.reshape(per, 4 * rows, LANES)

    all_to_all("update", fill_update, send_e, recv_e, e_send, e_recv)
    for t in range(2):
        block = g_full[t]
        left_term = dot(g_full[t, column(x), :], block, 1, 1)
        new_left_ref[t] = jnp.where(used[t] > 0.0, 0.95 * stat_l[t] + 0.05 * left_term, stat_l[t])
        right_term = dot(g_full[t, :, column(x)], block, 0, 0)
        new_right_ref[t] = jnp.where(used[t] > 0.0, 0.95 * stat_r[t] + 0.05 * right_term, stat_r[t])
    arrived("update")
    picked = dot(place[...], recv_e[...].reshape(chips * 4 * rows, LANES))
    update_ref[...] = picked.astype(BF16).reshape(layers, rows, blocks_per, LANES)
    finish()


def stay(array):
    return pltpu.with_memory_space_constraint(array, pltpu.HBM)


def store_kernel(*refs):
    count = (len(refs) - 1) // 2
    copies = [
        pltpu.make_async_copy(refs[i], refs[count + i], refs[-1].at[i]) for i in range(count)
    ]
    for copy in copies:
        copy.start()
    for copy in copies:
        copy.wait()


def local(gradient, owner_slot, stat_left, stat_right, second_moment, basis_left, basis_right):
    layers, row_dev, columns = gradient.shape[1:]
    capacity, quarter, order = basis_right.shape
    blocks_per = columns // order
    chips = LINE * LINE
    many = layers * blocks_per * row_dev
    vmem = pl.BlockSpec(memory_space=pltpu.VMEM)
    hbm = pl.BlockSpec(memory_space=pltpu.HBM)
    dma = pltpu.SemaphoreType.DMA
    message = (chips, 4 * row_dev, quarter)
    stat = (capacity, quarter, order)
    full = (capacity, order, order)
    results = pl.pallas_call(
        kernel,
        name="soap_step",
        out_shape=(
            pltpu.VMEM((layers, row_dev, blocks_per, quarter), BF16),
            pltpu.VMEM(stat, F32),
            pltpu.VMEM(stat, F32),
            pltpu.VMEM(stat, F32),
        ),
        in_specs=[hbm] * 7,
        out_specs=[vmem] * 4,
        scratch_shapes=[
            pltpu.VMEM(owner_slot.shape, I32),
            pltpu.VMEM(gradient.shape[1:], BF16),
            pltpu.VMEM((4, many, quarter), BF16),
            pltpu.VMEM((3, many, quarter), BF16),
            pltpu.VMEM((2, many, quarter), BF16),
            pltpu.VMEM((chips * 2 * row_dev, many), BF16),
            pltpu.VMEM((many, chips * 4 * row_dev), BF16),
            pltpu.VMEM((256, 256), BF16),
            pltpu.VMEM((256, 256), BF16),
            pltpu.VMEM((256, 256), BF16),
            pltpu.VMEM(message, BF16),
            pltpu.VMEM(message, BF16),
            pltpu.VMEM(full, BF16),
            pltpu.VMEM(full, BF16),
            pltpu.VMEM(full, BF16),
            pltpu.VMEM((capacity, order, quarter), BF16),
            pltpu.VMEM((capacity, quarter, order), BF16),
            pltpu.VMEM(stat, F32),
            pltpu.VMEM((capacity, quarter, order), BF16),
            pltpu.VMEM((capacity, order, quarter), BF16),
            pltpu.VMEM((capacity, order, quarter), BF16),
            pltpu.VMEM((capacity, order, quarter), BF16),
            pltpu.VMEM(message, BF16),
            pltpu.VMEM(message, BF16),
            pltpu.VMEM(stat, F32),
            pltpu.VMEM(stat, F32),
            pltpu.VMEM(stat, F32),
            dma((10,)),
            dma, dma((2,)),
            dma, dma((2,)),
            dma, dma,
            dma, dma((2,)), dma((2,)),
            dma, dma, dma,
            dma, dma, dma,
            dma, dma((2,)),
            dma, dma((2,)),
            dma, dma,
            pltpu.SemaphoreType.REGULAR((5,)),
        ],
        compiler_params=pltpu.CompilerParams(
            collective_id=0, has_side_effects=True, vmem_limit_bytes=40 << 20
        ),
    )(*(stay(a) for a in (owner_slot, gradient[0], stat_left, stat_right, second_moment, basis_left, basis_right)))
    return pl.pallas_call(
        store_kernel,
        name="store",
        out_shape=tuple(jax.ShapeDtypeStruct(r.shape, r.dtype) for r in results),
        in_specs=[vmem] * 4,
        out_specs=[hbm] * 4,
        scratch_shapes=[dma((4,))],
        compiler_params=pltpu.CompilerParams(vmem_limit_bytes=8 << 20),
    )(*results)


def solution(mesh):
    placed = (
        P("dp", None, "fsdp", None),
        P(),
        P("fsdp", "dp", None),
        P("fsdp", "dp", None),
        P("fsdp", "dp", None),
        P("fsdp", None, "dp"),
        P("fsdp", "dp", None),
    )
    return jax.shard_map(
        local,
        mesh=mesh,
        in_specs=placed,
        out_specs=(
            P(None, "fsdp", None, "dp"),
            P("fsdp", "dp", None),
            P("fsdp", "dp", None),
            P("fsdp", "dp", None),
        ),
        check_vma=False,
    )
```

```python
import functools

import jax
import jax.numpy as jnp
from jax import lax
from jax.experimental import pallas as pl
from jax.experimental.pallas import tpu as pltpu
from jax.sharding import PartitionSpec as P

epsilon = 1e-08
MESH = pl.DeviceIdType.MESH
F32, BF16, I32 = jnp.float32, jnp.bfloat16, jnp.int32
LINE = 8
LANES = 128


def hops(d):
    return min(d, LINE - d)


far_first = sorted(
    ((dz, dy) for dz in range(LINE) for dy in range(LINE) if dz or dy),
    key=lambda step: -hops(step[0]) - hops(step[1]),
)


def iota(shape, dim):
    return lax.broadcasted_iota(I32, shape, dim)


def dot(a, b, ca=1, cb=0):
    return lax.dot_general(a, b, (((ca,), (cb,)), ((), ())), preferred_element_type=F32)


def one_hot(rows, columns):
    return jnp.where(rows == columns, 1.0, 0.0).astype(BF16)


def kernel(
    slot_ref, grad_ref, left_ref, right_ref, moment_ref, bl_ref, br_ref,
    recv_e, place, new_left_ref, new_right_ref, new_moment_ref,
    slot_vmem, grad, parted, raw, mean, pick, sort_in, sort_own, sort_sib,
    send_b, recv_b, g_full, l_full, r_full, l_own, l_turned, rotated_ref, back_own, back_full,
    out_own, out_sib, send_e, stat_l, stat_r, stat_m,
    local_sem, a_send, a_recv, x_send, x_recv, b_send, b_recv, c_send, c_near, c_far,
    l_send, l_near, l_far, r_send, r_near, r_far, d_send, d_recv, y_send, y_recv,
    e_send, e_recv, tokens,
):
    x = lax.axis_index("dp")
    f = lax.axis_index("fsdp")
    groups = 4
    core = lax.rem(f, 2)
    chip = f // 2
    z, y = chip // LINE, lax.rem(chip, LINE)
    chips = LINE * LINE
    sibling = (x, f + 1 - 2 * core)
    layers, rows, columns = grad_ref.shape
    order = g_full.shape[1]
    blocks_per = columns // order
    many = layers * rows * blocks_per
    quarter = order // groups
    half = quarter // 2
    parts = pl.ds(0, order - quarter)

    def x_peer(d):
        return lax.rem(x + d + groups, groups)

    def device(zz, yy):
        return (x, (zz * LINE + yy) * 2 + core)

    def z_peer(d):
        return device(lax.rem(z + d + LINE, LINE), y)

    def y_peer(d):
        return device(z, lax.rem(y + d + LINE, LINE))

    def column(p):
        return pl.ds(pl.multiple_of(p * LANES, LANES), LANES)

    def row_half(p, size, which):
        return pl.ds(pl.multiple_of(p * size + which * (size // 2), size // 2), size // 2)

    def remote(src, dst, send, recv, to):
        return pltpu.make_async_remote_copy(
            src_ref=src, dst_ref=dst, send_sem=send, recv_sem=recv,
            device_id=to, device_id_type=MESH,
        )

    def signal(sem, to):
        pl.semaphore_signal(sem, inc=1, device_id=to, device_id_type=MESH)

    pending = {}

    def started(name, ref, sem):
        pending[name] = lambda: pltpu.make_async_copy(ref, ref, sem).wait()

    def arrived(name):
        pending.pop(name)()

    def finish():
        for name in list(pending):
            arrived(name)

    barrier = pltpu.get_barrier_semaphore()
    for d in (2, 1, -1):
        signal(barrier, (x_peer(d), f))
    for d in (1, -1):
        signal(barrier, z_peer(d))
        signal(barrier, y_peer(d))
    signal(barrier, sibling)

    loads = [
        pltpu.make_async_copy(slot_ref, slot_vmem, local_sem.at[0]),
        pltpu.make_async_copy(grad_ref, grad, local_sem.at[1]),
        pltpu.make_async_copy(bl_ref, l_own, local_sem.at[2]),
        pltpu.make_async_copy(left_ref, stat_l, local_sem.at[3]),
        pltpu.make_async_copy(right_ref, stat_r, local_sem.at[4]),
        pltpu.make_async_copy(moment_ref, stat_m, local_sem.at[5]),
    ]
    for t in range(2):
        loads.append(pltpu.make_async_copy(bl_ref.at[t], l_full.at[t, :, column(x)], local_sem.at[6 + t]))
        loads.append(pltpu.make_async_copy(br_ref.at[t], r_full.at[t, column(x), :], local_sem.at[8 + t]))
    loads[1].start()
    for i, load in enumerate(loads):
        if i != 1:
            load.start()
        pending["load", i] = load.wait
    def cut(at, d, h):
        p = x_peer(d)
        for l in range(h * some, (h + 1) * some):
            pieces = [
                grad[l, :, pl.ds(pl.multiple_of(c * order + p * LANES, LANES), LANES)].astype(F32)
                for c in range(blocks_per)
            ]
            size = rows * blocks_per
            parted[at, l * size : (l + 1) * size] = jnp.concatenate(pieces, axis=0).astype(BF16)

    some = layers // 2
    peers = ((1, 2), (0, 1), (2, -1))
    arrived(("load", 1))
    cut(*peers[0], 0)
    pl.semaphore_wait(barrier, 8)

    def greet(i, peers):
        for d in (1, -1):
            signal(tokens.at[i], peers(d * (2 if i in (1, 4) else 1)))
        pending["token", i] = lambda: pl.semaphore_wait(tokens.at[i], 2)

    greet(0, z_peer)

    for h in range(2):
        held = pl.ds(h * (many // 2), many // 2)
        for at, d in peers:
            if (at, h) != (peers[0][0], 0):
                cut(at, d, h)
            remote(
                parted.at[at, held], raw.at[at, held], a_send, a_recv.at[h], (x_peer(d), f)
            ).start()
        started(("groups", h), raw.at[pl.ds(0, 3), held], a_recv.at[h])
    started("groups sent", raw.at[pl.ds(0, 3)], a_send)
    for h in range(2):
        cut(3, 0, h)

    for i in range(6, 10):
        arrived(("load", i))
    for t in range(2):
        for d in (1, -1):
            mine = r_full.at[t, column(x), :]
            remote(mine, mine, r_send, r_near, (x_peer(d), f)).start()
    near_rows = pl.ds(0, 2 * quarter)
    started("right near", r_full.at[:, near_rows, :], r_near)
    started("right sent", r_full.at[:, near_rows, :], r_send)

    arrived(("load", 0))
    slots = slot_vmem[...].astype(F32).astype(BF16)
    spread = one_hot(lax.rem(iota((blocks_per, many), 1) // rows, blocks_per), iota((blocks_per, many), 0))
    wide = dot(slots, spread)
    own_layer = iota((layers, many), 1) // (rows * blocks_per) == iota((layers, many), 0)
    slot_lane = jnp.sum(jnp.where(own_layer, wide, 0.0), axis=0, keepdims=True).astype(I32)
    row_lane = lax.rem(iota((1, many), 1), rows)
    owner_lane = slot_lane // 2
    code_lane = jnp.where(
        lax.rem(owner_lane, 2) == core,
        (owner_lane // 2) * 2 * rows + lax.rem(slot_lane, 2) * rows + row_lane, -1,
    )
    used = [jnp.max(jnp.where(slot_lane == 2 * f + t, 1.0, 0.0), axis=1, keepdims=True) for t in range(2)]
    pick[...] = one_hot(code_lane, iota((chips * 2 * rows, many), 0))
    arrived(("token", 0))
    greet(1, z_peer)
    tall_spread = one_hot(lax.rem(iota((many, blocks_per), 0), blocks_per), iota((many, blocks_per), 1))
    tall = dot(tall_spread, slots, 1, 1)
    tall_layer = iota((many, layers), 0) // (rows * blocks_per) == iota((many, layers), 1)
    slot_col = jnp.sum(jnp.where(tall_layer, tall, 0.0), axis=1, keepdims=True).astype(I32)
    row_col = lax.rem(iota((many, 1), 0) // blocks_per, rows)
    owner_col = slot_col // 2
    far = jnp.where(lax.rem(owner_col, 2) == core, 0, 1)
    code_col = ((owner_col // 2) * 2 + far) * 2 * rows + lax.rem(slot_col, 2) * rows + row_col
    place[...] = one_hot(code_col, iota((many, chips * 4 * rows), 1))
    arrived(("token", 1))
    greet(2, y_peer)
    chunk = 256
    part = chunk // 2
    per = chunk // (4 * rows)
    ro, co = iota((chunk, 1), 0), iota((1, chunk), 1)
    far_o = lax.rem(lax.rem(ro // rows, 2) + core, 2)
    want = ((lax.rem(ro // (2 * rows), per) * 2 + far_o) * 2 + ro // part) * rows + lax.rem(ro, rows)
    sort_in[...] = one_hot(want, co)
    chip_o = ro // (4 * rows)
    t_o = lax.rem(ro // rows, 2)
    want = ((t_o * per + chip_o) * 2 + core) * rows + lax.rem(ro, rows)
    far_o = lax.rem(ro // (2 * rows), 2)
    sort_own[...] = one_hot(jnp.where(far_o == 0, want, -1), co)
    sort_sib[...] = one_hot(jnp.where(far_o == 1, want, -1), co)
    arrived(("token", 2))
    greet(3, y_peer)
    for i in range(2, 6):
        arrived(("load", i))
    for t in range(2):
        l_turned[t] = l_own[t].astype(F32).T.astype(BF16)

    def add_groups(h):
        arrived(("groups", h))
        lines = pl.ds(h * (many // 2), many // 2)
        total = parted[3, lines].astype(F32)
        for g in range(groups - 1):
            total = total + raw[g, lines].astype(F32)
        mean[0, lines] = (total * (1.0 / groups)).astype(BF16)
        remote(mean.at[0, lines], mean.at[1, lines], x_send, x_recv.at[h], sibling).start()
        started(("mean", h), mean.at[1, lines], x_recv.at[h])
        started("mean sent", mean.at[0, pl.ds(0, (h + 1) * (many // 2))], x_send)

    add_groups(0)
    arrived(("token", 3))
    greet(4, y_peer)
    arrived("groups sent")
    for t in range(2):
        for d in (1, -1):
            mine = l_full.at[t, :, column(x)]
            remote(mine, mine, l_send, l_near, (x_peer(d), f)).start()
    started("left near", l_full.at[:, near_rows, :], l_near)
    started("left sent", l_full.at[:, near_rows, :], l_send)

    add_groups(1)
    near = [dot(pick[j * part : (j + 1) * part], mean[0]) for j in range(LINE // 2)]
    arrived(("mean", 0))
    arrived(("mean", 1))

    arrived(("token", 4))

    along_z = [lax.rem(z + d, LINE) for d in range(LINE)]
    along_y = [lax.rem(y + d, LINE) for d in range(LINE)]

    def all_to_all(name, fill, src, dst, send, recv):
        for j in range(LINE // 2):
            fill(j)
        for dz, dy in far_first:
            to = along_z[dz] * LINE + along_y[dy]
            remote(src.at[to], dst.at[chip], send, recv, (x, to * 2 + core)).start()
        dst[chip] = src[chip]
        started(name, dst.at[pl.ds(0, chips - 1)], recv)
        started(name + " sent", src.at[pl.ds(0, chips - 1)], send)

    def fill_rows(j):
        away = dot(pick[j * part : (j + 1) * part], mean[1])
        both = [v.reshape(per, 2 * rows, LANES) for v in (near[j], away)]
        send_b[j * per : (j + 1) * per] = jnp.concatenate(both, axis=1).astype(BF16)

    all_to_all("rows", fill_rows, send_b, recv_b, b_send, b_recv)

    arrived("right near")
    for t in range(2):
        for i, d in enumerate((1, -1)):
            piece = r_full.at[t, row_half(x_peer(-d), quarter, i), :]
            remote(piece, piece, r_send, r_far, (x_peer(d), f)).start()
    started("right", r_full.at[:, pl.ds(0, quarter), :], r_far)
    started("right sent", r_full.at[:, parts, :], r_send)

    arrived("rows")
    for j in range(chips // per):
        rows_j = dot(sort_in[...], recv_b[j * per : (j + 1) * per].reshape(chunk, LANES)).astype(BF16)
        for t in range(2):
            g_full[t, j * part : (j + 1) * part, column(x)] = rows_j[t * part : (t + 1) * part]
    for t in range(2):
        for d in (1, -1):
            mine = g_full.at[t, :, column(x)]
            remote(mine, mine, c_send, c_near.at[t], (x_peer(d), f)).start()
        started(("block near", t), g_full.at[t, pl.ds(0, 2 * quarter), :], c_near.at[t])
    started("blocks sent", g_full.at[:, pl.ds(0, 2 * quarter), :], c_send)
    for t in range(2):
        arrived(("block near", t))
        for i, d in enumerate((1, -1)):
            piece = g_full.at[t, pl.ds(i * (order // 2), order // 2), column(x_peer(-d))]
            remote(piece, piece, c_send, c_far.at[t], (x_peer(d), f)).start()
        started(("block", t), g_full.at[t, pl.ds(0, quarter), :], c_far.at[t])
    started("blocks sent", g_full.at[:, parts, :], c_send)
    arrived("left near")
    for t in range(2):
        for i, d in enumerate((1, -1)):
            piece = l_full.at[t, pl.ds(i * (order // 2), order // 2), column(x_peer(-d))]
            remote(piece, piece, l_send, l_far, (x_peer(d), f)).start()
    started("left", l_full.at[:, pl.ds(0, quarter), :], l_far)
    started("left sent", l_full.at[:, parts, :], l_send)
    arrived("right")

    def turn(t, pieces):
        total = 0.0
        for p in pieces:
            half_turn = dot(l_turned[t], g_full[t, :, column(p)]).astype(BF16)
            total = total + dot(half_turn, r_full[t, column(p), :])
        return total

    for t in range(2):
        rotated_ref[t] = turn(t, (x, x_peer(1), x_peer(-1)))

    def block_step(t):
        rotated = rotated_ref[t] + turn(t, (x_peer(2),))
        right = r_full[t]
        moment = 0.95 * stat_m[t] + 0.05 * rotated * rotated
        new_moment_ref[t] = jnp.where(used[t] > 0.0, moment, stat_m[t])
        scaled = (rotated / (jnp.sqrt(moment) + epsilon)).astype(BF16)
        back_own[t] = dot(scaled, right, 1, 1).astype(BF16)
        for d in (2, 1, -1):
            p = x_peer(d)
            remote(
                back_own.at[t, :, column(p)], back_full.at[t, column(x), :],
                d_send, d_recv.at[t], (p, f),
            ).start()
        started(("back", t), back_full.at[t, parts, :], d_recv.at[t])
        started("back sent", back_full.at[pl.ds(0, t + 1), parts, :], d_send)
        back_full[t, column(x), :] = back_own[t, :, column(x)]

    def out_step(t):
        arrived(("back", t))
        out_own[t] = dot(l_full[t], back_full[t]).astype(BF16)
        remote(out_own.at[t], out_sib.at[t], y_send, y_recv.at[t], sibling).start()
        started(("out", t), out_sib.at[t], y_recv.at[t])
        started("out sent", out_own.at[pl.ds(0, t + 1)], y_send)

    arrived(("block", 0))
    block_step(0)
    arrived(("block", 1))
    block_step(1)
    arrived("left")
    out_step(0)
    out_step(1)
    def sort_rows(ref, sort, j):
        both = jnp.concatenate([ref[t, j * part : (j + 1) * part] for t in range(2)], axis=0)
        return dot(sort[...], both)

    mine = [sort_rows(out_own, sort_own, j) for j in range(LINE // 2)]
    arrived(("out", 0))
    arrived(("out", 1))

    def fill_update(j):
        both = (mine[j] + sort_rows(out_sib, sort_sib, j)).astype(BF16)
        send_e[j * per : (j + 1) * per] = both.reshape(per, 4 * rows, LANES)

    all_to_all("update", fill_update, send_e, recv_e, e_send, e_recv)
    for t in range(2):
        block = g_full[t]
        left_term = dot(g_full[t, column(x), :], block, 1, 1)
        new_left_ref[t] = jnp.where(used[t] > 0.0, 0.95 * stat_l[t] + 0.05 * left_term, stat_l[t])
        right_term = dot(g_full[t, :, column(x)], block, 0, 0)
        new_right_ref[t] = jnp.where(used[t] > 0.0, 0.95 * stat_r[t] + 0.05 * right_term, stat_r[t])
    arrived("update")
    finish()


def stay(array):
    return pltpu.with_memory_space_constraint(array, pltpu.HBM)


def store_kernel(
    rows_ref, place_ref, left_ref, right_ref, moment_ref,
    update_ref, new_left_ref, new_right_ref, new_moment_ref, update, semaphores,
):
    pairs = ((left_ref, new_left_ref), (right_ref, new_right_ref), (moment_ref, new_moment_ref))
    copies = [
        pltpu.make_async_copy(src, dst, semaphores.at[i]) for i, (src, dst) in enumerate(pairs)
    ]
    for copy in copies:
        copy.start()
    picked = dot(place_ref[...], rows_ref[...].reshape(place_ref.shape[1], LANES))
    update[...] = picked.astype(BF16).reshape(update.shape)
    copies.append(pltpu.make_async_copy(update, update_ref, semaphores.at[3]))
    copies[3].start()
    for copy in copies:
        copy.wait()


def local(gradient, owner_slot, stat_left, stat_right, second_moment, basis_left, basis_right):
    layers, row_dev, columns = gradient.shape[1:]
    capacity, quarter, order = basis_right.shape
    blocks_per = columns // order
    chips = LINE * LINE
    many = layers * blocks_per * row_dev
    vmem = pl.BlockSpec(memory_space=pltpu.VMEM)
    hbm = pl.BlockSpec(memory_space=pltpu.HBM)
    dma = pltpu.SemaphoreType.DMA
    message = (chips, 4 * row_dev, quarter)
    stat = (capacity, quarter, order)
    full = (capacity, order, order)
    results = pl.pallas_call(
        kernel,
        name="soap_step",
        out_shape=(
            pltpu.VMEM(message, BF16),
            pltpu.VMEM((many, chips * 4 * row_dev), BF16),
            pltpu.VMEM(stat, F32),
            pltpu.VMEM(stat, F32),
            pltpu.VMEM(stat, F32),
        ),
        in_specs=[hbm] * 7,
        out_specs=[vmem] * 5,
        scratch_shapes=[
            pltpu.VMEM(owner_slot.shape, I32),
            pltpu.VMEM(gradient.shape[1:], BF16),
            pltpu.VMEM((4, many, quarter), BF16),
            pltpu.VMEM((3, many, quarter), BF16),
            pltpu.VMEM((2, many, quarter), BF16),
            pltpu.VMEM((chips * 2 * row_dev, many), BF16),
            pltpu.VMEM((256, 256), BF16),
            pltpu.VMEM((256, 256), BF16),
            pltpu.VMEM((256, 256), BF16),
            pltpu.VMEM(message, BF16),
            pltpu.VMEM(message, BF16),
            pltpu.VMEM(full, BF16),
            pltpu.VMEM(full, BF16),
            pltpu.VMEM(full, BF16),
            pltpu.VMEM((capacity, order, quarter), BF16),
            pltpu.VMEM((capacity, quarter, order), BF16),
            pltpu.VMEM(stat, F32),
            pltpu.VMEM((capacity, quarter, order), BF16),
            pltpu.VMEM((capacity, order, quarter), BF16),
            pltpu.VMEM((capacity, order, quarter), BF16),
            pltpu.VMEM((capacity, order, quarter), BF16),
            pltpu.VMEM(message, BF16),
            pltpu.VMEM(stat, F32),
            pltpu.VMEM(stat, F32),
            pltpu.VMEM(stat, F32),
            dma((10,)),
            dma, dma((2,)),
            dma, dma((2,)),
            dma, dma,
            dma, dma((2,)), dma((2,)),
            dma, dma, dma,
            dma, dma, dma,
            dma, dma((2,)),
            dma, dma((2,)),
            dma, dma,
            pltpu.SemaphoreType.REGULAR((5,)),
        ],
        compiler_params=pltpu.CompilerParams(
            collective_id=0, has_side_effects=True, vmem_limit_bytes=40 << 20
        ),
    )(*(stay(a) for a in (owner_slot, gradient[0], stat_left, stat_right, second_moment, basis_left, basis_right)))
    return pl.pallas_call(
        store_kernel,
        name="store",
        out_shape=(
            jax.ShapeDtypeStruct((layers, row_dev, blocks_per, quarter), BF16),
            *(jax.ShapeDtypeStruct(stat, F32) for _ in range(3)),
        ),
        in_specs=[vmem] * 5,
        out_specs=[hbm] * 4,
        scratch_shapes=[
            pltpu.VMEM((layers, row_dev, blocks_per, quarter), BF16),
            dma((4,)),
        ],
        compiler_params=pltpu.CompilerParams(vmem_limit_bytes=8 << 20),
    )(*results)


def solution(mesh):
    placed = (
        P("dp", None, "fsdp", None),
        P(),
        P("fsdp", "dp", None),
        P("fsdp", "dp", None),
        P("fsdp", "dp", None),
        P("fsdp", None, "dp"),
        P("fsdp", "dp", None),
    )
    return jax.shard_map(
        local,
        mesh=mesh,
        in_specs=placed,
        out_specs=(
            P(None, "fsdp", None, "dp"),
            P("fsdp", "dp", None),
            P("fsdp", "dp", None),
            P("fsdp", "dp", None),
        ),
        check_vma=False,
    )
```

```python
import functools

import jax
import jax.numpy as jnp
from jax import lax
from jax.experimental import pallas as pl
from jax.experimental.pallas import tpu as pltpu
from jax.sharding import PartitionSpec as P

epsilon = 1e-08
MESH = pl.DeviceIdType.MESH
F32, BF16, I32 = jnp.float32, jnp.bfloat16, jnp.int32
LINE = 8
LANES = 128


def hops(d):
    return min(d, LINE - d)


far_first = sorted(
    ((dz, dy) for dz in range(LINE) for dy in range(LINE) if dz or dy),
    key=lambda step: -hops(step[0]) - hops(step[1]),
)


def iota(shape, dim):
    return lax.broadcasted_iota(I32, shape, dim)


def dot(a, b, ca=1, cb=0):
    return lax.dot_general(a, b, (((ca,), (cb,)), ((), ())), preferred_element_type=F32)


def one_hot(rows, columns):
    return jnp.where(rows == columns, 1.0, 0.0).astype(BF16)


def kernel(
    slot_ref, grad_ref, left_ref, right_ref, moment_ref, bl_ref, br_ref,
    recv_e, place, new_left_ref, new_right_ref, new_moment_ref,
    slot_vmem, grad, parted, raw, mean, pick, sort_in, sort_own, sort_sib,
    send_b, recv_b, g_full, l_full, r_full, l_own, l_turned, rotated_ref, back_own, back_full,
    out_own, out_sib, send_e, stat_l, stat_r, stat_m,
    local_sem, a_send, a_recv, x_send, x_recv, b_send, b_recv, c_send, c_near, c_far,
    l_send, l_near, l_far, r_send, r_near, r_far, d_send, d_recv, y_send, y_recv,
    e_send, e_recv, tokens,
):
    x = lax.axis_index("dp")
    f = lax.axis_index("fsdp")
    groups = 4
    core = lax.rem(f, 2)
    chip = f // 2
    z, y = chip // LINE, lax.rem(chip, LINE)
    chips = LINE * LINE
    sibling = (x, f + 1 - 2 * core)
    layers, rows, columns = grad_ref.shape
    order = g_full.shape[1]
    blocks_per = columns // order
    many = layers * rows * blocks_per
    quarter = order // groups
    half = quarter // 2
    parts = pl.ds(0, order - quarter)

    def x_peer(d):
        return lax.rem(x + d + groups, groups)

    def device(zz, yy):
        return (x, (zz * LINE + yy) * 2 + core)

    def z_peer(d):
        return device(lax.rem(z + d + LINE, LINE), y)

    def y_peer(d):
        return device(z, lax.rem(y + d + LINE, LINE))

    def column(p):
        return pl.ds(pl.multiple_of(p * LANES, LANES), LANES)

    def row_half(p, size, which):
        return pl.ds(pl.multiple_of(p * size + which * (size // 2), size // 2), size // 2)

    def remote(src, dst, send, recv, to):
        return pltpu.make_async_remote_copy(
            src_ref=src, dst_ref=dst, send_sem=send, recv_sem=recv,
            device_id=to, device_id_type=MESH,
        )

    def signal(sem, to):
        pl.semaphore_signal(sem, inc=1, device_id=to, device_id_type=MESH)

    pending = {}

    def started(name, ref, sem):
        pending[name] = lambda: pltpu.make_async_copy(ref, ref, sem).wait()

    def arrived(name):
        pending.pop(name)()

    def finish():
        for name in list(pending):
            arrived(name)

    barrier = pltpu.get_barrier_semaphore()
    for d in (2, 1, -1):
        signal(barrier, (x_peer(d), f))
    for d in (1, -1):
        signal(barrier, z_peer(d))
        signal(barrier, y_peer(d))
    signal(barrier, sibling)

    loads = [
        pltpu.make_async_copy(slot_ref, slot_vmem, local_sem.at[0]),
        pltpu.make_async_copy(grad_ref, grad, local_sem.at[1]),
        pltpu.make_async_copy(bl_ref, l_own, local_sem.at[2]),
        pltpu.make_async_copy(left_ref, stat_l, local_sem.at[3]),
        pltpu.make_async_copy(right_ref, stat_r, local_sem.at[4]),
        pltpu.make_async_copy(moment_ref, stat_m, local_sem.at[5]),
    ]
    for t in range(2):
        loads.append(pltpu.make_async_copy(bl_ref.at[t], l_full.at[t, :, column(x)], local_sem.at[6 + t]))
        loads.append(pltpu.make_async_copy(br_ref.at[t], r_full.at[t, column(x), :], local_sem.at[8 + t]))
    loads[1].start()
    for i, load in enumerate(loads):
        if i != 1:
            load.start()
        pending["load", i] = load.wait
    def cut(at, d, h):
        p = x_peer(d)
        for l in range(h * some, (h + 1) * some):
            pieces = [
                grad[l, :, pl.ds(pl.multiple_of(c * order + p * LANES, LANES), LANES)].astype(F32)
                for c in range(blocks_per)
            ]
            size = rows * blocks_per
            parted[at, l * size : (l + 1) * size] = jnp.concatenate(pieces, axis=0).astype(BF16)

    some = layers // 2
    peers = ((1, 2), (0, 1), (2, -1))
    arrived(("load", 1))
    cut(*peers[0], 0)
    pl.semaphore_wait(barrier, 8)

    def greet(i, peers):
        for d in (1, -1):
            signal(tokens.at[i], peers(d * (2 if i in (1, 4) else 1)))
        pending["token", i] = lambda: pl.semaphore_wait(tokens.at[i], 2)

    greet(0, z_peer)

    for h in range(2):
        held = pl.ds(h * (many // 2), many // 2)
        for at, d in peers:
            if (at, h) != (peers[0][0], 0):
                cut(at, d, h)
            remote(
                parted.at[at, held], raw.at[at, held], a_send, a_recv.at[h], (x_peer(d), f)
            ).start()
        started(("groups", h), raw.at[pl.ds(0, 3), held], a_recv.at[h])
    started("groups sent", raw.at[pl.ds(0, 3)], a_send)
    for h in range(2):
        cut(3, 0, h)

    for i in range(6, 10):
        arrived(("load", i))
    for t in range(2):
        for d in (1, -1):
            mine = r_full.at[t, column(x), :]
            remote(mine, mine, r_send, r_near, (x_peer(d), f)).start()
    near_rows = pl.ds(0, 2 * quarter)
    started("right near", r_full.at[:, near_rows, :], r_near)
    started("right sent", r_full.at[:, near_rows, :], r_send)

    arrived(("load", 0))
    slots = slot_vmem[...].astype(F32).astype(BF16)
    spread = one_hot(lax.rem(iota((blocks_per, many), 1) // rows, blocks_per), iota((blocks_per, many), 0))
    wide = dot(slots, spread)
    own_layer = iota((layers, many), 1) // (rows * blocks_per) == iota((layers, many), 0)
    slot_lane = jnp.sum(jnp.where(own_layer, wide, 0.0), axis=0, keepdims=True).astype(I32)
    row_lane = lax.rem(iota((1, many), 1), rows)
    owner_lane = slot_lane // 2
    code_lane = jnp.where(
        lax.rem(owner_lane, 2) == core,
        (owner_lane // 2) * 2 * rows + lax.rem(slot_lane, 2) * rows + row_lane, -1,
    )
    used = [jnp.max(jnp.where(slot_lane == 2 * f + t, 1.0, 0.0), axis=1, keepdims=True) for t in range(2)]
    pick[...] = one_hot(code_lane, iota((chips * 2 * rows, many), 0))
    arrived(("token", 0))
    greet(1, z_peer)
    tall_spread = one_hot(lax.rem(iota((many, blocks_per), 0), blocks_per), iota((many, blocks_per), 1))
    tall = dot(tall_spread, slots, 1, 1)
    tall_layer = iota((many, layers), 0) // (rows * blocks_per) == iota((many, layers), 1)
    slot_col = jnp.sum(jnp.where(tall_layer, tall, 0.0), axis=1, keepdims=True).astype(I32)
    row_col = lax.rem(iota((many, 1), 0) // blocks_per, rows)
    owner_col = slot_col // 2
    far = jnp.where(lax.rem(owner_col, 2) == core, 0, 1)
    code_col = ((owner_col // 2) * 2 + far) * 2 * rows + lax.rem(slot_col, 2) * rows + row_col
    place[...] = one_hot(code_col, iota((many, chips * 4 * rows), 1))
    arrived(("token", 1))
    greet(2, y_peer)
    chunk = 256
    part = chunk // 2
    per = chunk // (4 * rows)
    ro, co = iota((chunk, 1), 0), iota((1, chunk), 1)
    far_o = lax.rem(lax.rem(ro // rows, 2) + core, 2)
    want = ((lax.rem(ro // (2 * rows), per) * 2 + far_o) * 2 + ro // part) * rows + lax.rem(ro, rows)
    sort_in[...] = one_hot(want, co)
    chip_o = ro // (4 * rows)
    t_o = lax.rem(ro // rows, 2)
    want = ((t_o * per + chip_o) * 2 + core) * rows + lax.rem(ro, rows)
    far_o = lax.rem(ro // (2 * rows), 2)
    sort_own[...] = one_hot(jnp.where(far_o == 0, want, -1), co)
    sort_sib[...] = one_hot(jnp.where(far_o == 1, want, -1), co)
    arrived(("token", 2))
    greet(3, y_peer)
    for i in range(2, 6):
        arrived(("load", i))
    for t in range(2):
        l_turned[t] = l_own[t].astype(F32).T.astype(BF16)

    def add_groups(h):
        arrived(("groups", h))
        lines = pl.ds(h * (many // 2), many // 2)
        total = parted[3, lines].astype(F32)
        for g in range(groups - 1):
            total = total + raw[g, lines].astype(F32)
        mean[0, lines] = (total * (1.0 / groups)).astype(BF16)
        remote(mean.at[0, lines], mean.at[1, lines], x_send, x_recv.at[h], sibling).start()
        started(("mean", h), mean.at[1, lines], x_recv.at[h])
        started("mean sent", mean.at[0, pl.ds(0, (h + 1) * (many // 2))], x_send)

    add_groups(0)
    arrived(("token", 3))
    greet(4, y_peer)
    arrived("groups sent")
    for t in range(2):
        for d in (1, -1):
            mine = l_full.at[t, :, column(x)]
            remote(mine, mine, l_send, l_near, (x_peer(d), f)).start()
    started("left near", l_full.at[:, near_rows, :], l_near)
    started("left sent", l_full.at[:, near_rows, :], l_send)

    add_groups(1)
    near = [dot(pick[j * part : (j + 1) * part], mean[0]) for j in range(LINE // 2)]
    arrived(("mean", 0))
    arrived(("mean", 1))

    arrived(("token", 4))

    along_z = [lax.rem(z + d, LINE) for d in range(LINE)]
    along_y = [lax.rem(y + d, LINE) for d in range(LINE)]

    def all_to_all(name, fill, src, dst, send, recv):
        for j in range(LINE // 2):
            fill(j)
        for dz, dy in far_first:
            to = along_z[dz] * LINE + along_y[dy]
            remote(src.at[to], dst.at[chip], send, recv, (x, to * 2 + core)).start()
        dst[chip] = src[chip]
        started(name, dst.at[pl.ds(0, chips - 1)], recv)
        started(name + " sent", src.at[pl.ds(0, chips - 1)], send)

    def fill_rows(j):
        away = dot(pick[j * part : (j + 1) * part], mean[1])
        both = [v.reshape(per, 2 * rows, LANES) for v in (near[j], away)]
        send_b[j * per : (j + 1) * per] = jnp.concatenate(both, axis=1).astype(BF16)

    all_to_all("rows", fill_rows, send_b, recv_b, b_send, b_recv)

    arrived("right near")
    for t in range(2):
        for i, d in enumerate((1, -1)):
            piece = r_full.at[t, row_half(x_peer(-d), quarter, i), :]
            remote(piece, piece, r_send, r_far, (x_peer(d), f)).start()
    started("right", r_full.at[:, pl.ds(0, quarter), :], r_far)
    started("right sent", r_full.at[:, parts, :], r_send)

    arrived("rows")
    for t in range(2):
        for j in range(chips // per):
            rows_j = recv_b[j * per : (j + 1) * per].reshape(chunk, LANES)
            sorted_j = dot(sort_in[t * part : (t + 1) * part], rows_j)
            g_full[t, j * part : (j + 1) * part, column(x)] = sorted_j.astype(BF16)
        for d in (1, -1):
            mine = g_full.at[t, :, column(x)]
            remote(mine, mine, c_send, c_near.at[t], (x_peer(d), f)).start()
        started(("block near", t), g_full.at[t, pl.ds(0, 2 * quarter), :], c_near.at[t])
    started("blocks sent", g_full.at[:, pl.ds(0, 2 * quarter), :], c_send)
    for t in range(2):
        arrived(("block near", t))
        for i, d in enumerate((1, -1)):
            piece = g_full.at[t, pl.ds(i * (order // 2), order // 2), column(x_peer(-d))]
            remote(piece, piece, c_send, c_far.at[t], (x_peer(d), f)).start()
        started(("block", t), g_full.at[t, pl.ds(0, quarter), :], c_far.at[t])
    started("blocks sent", g_full.at[:, parts, :], c_send)
    arrived("left near")
    for t in range(2):
        for i, d in enumerate((1, -1)):
            piece = l_full.at[t, pl.ds(i * (order // 2), order // 2), column(x_peer(-d))]
            remote(piece, piece, l_send, l_far, (x_peer(d), f)).start()
    started("left", l_full.at[:, pl.ds(0, quarter), :], l_far)
    started("left sent", l_full.at[:, parts, :], l_send)
    arrived("right")

    def turn(t, pieces):
        total = 0.0
        for p in pieces:
            half_turn = dot(l_turned[t], g_full[t, :, column(p)]).astype(BF16)
            total = total + dot(half_turn, r_full[t, column(p), :])
        return total

    for t in range(2):
        rotated_ref[t] = turn(t, (x, x_peer(1), x_peer(-1)))

    def block_step(t):
        rotated = rotated_ref[t] + turn(t, (x_peer(2),))
        right = r_full[t]
        moment = 0.95 * stat_m[t] + 0.05 * rotated * rotated
        new_moment_ref[t] = jnp.where(used[t] > 0.0, moment, stat_m[t])
        scaled = (rotated / (jnp.sqrt(moment) + epsilon)).astype(BF16)
        back_own[t] = dot(scaled, right, 1, 1).astype(BF16)
        for d in (2, 1, -1):
            p = x_peer(d)
            remote(
                back_own.at[t, :, column(p)], back_full.at[t, column(x), :],
                d_send, d_recv.at[t], (p, f),
            ).start()
        started(("back", t), back_full.at[t, parts, :], d_recv.at[t])
        started("back sent", back_full.at[pl.ds(0, t + 1), parts, :], d_send)
        back_full[t, column(x), :] = back_own[t, :, column(x)]

    def out_step(t):
        arrived(("back", t))
        out_own[t] = dot(l_full[t], back_full[t]).astype(BF16)
        remote(out_own.at[t], out_sib.at[t], y_send, y_recv.at[t], sibling).start()
        started(("out", t), out_sib.at[t], y_recv.at[t])
        started("out sent", out_own.at[pl.ds(0, t + 1)], y_send)

    arrived(("block", 0))
    block_step(0)
    arrived(("block", 1))
    block_step(1)
    arrived("left")
    out_step(0)
    out_step(1)
    def sort_rows(ref, sort, j):
        both = jnp.concatenate([ref[t, j * part : (j + 1) * part] for t in range(2)], axis=0)
        return dot(sort[...], both)

    mine = [sort_rows(out_own, sort_own, j) for j in range(LINE // 2)]
    arrived(("out", 0))
    arrived(("out", 1))

    def fill_update(j):
        both = (mine[j] + sort_rows(out_sib, sort_sib, j)).astype(BF16)
        send_e[j * per : (j + 1) * per] = both.reshape(per, 4 * rows, LANES)

    all_to_all("update", fill_update, send_e, recv_e, e_send, e_recv)
    for t in range(2):
        block = g_full[t]
        left_term = dot(g_full[t, column(x), :], block, 1, 1)
        new_left_ref[t] = jnp.where(used[t] > 0.0, 0.95 * stat_l[t] + 0.05 * left_term, stat_l[t])
        right_term = dot(g_full[t, :, column(x)], block, 0, 0)
        new_right_ref[t] = jnp.where(used[t] > 0.0, 0.95 * stat_r[t] + 0.05 * right_term, stat_r[t])
    arrived("update")
    finish()


def stay(array):
    return pltpu.with_memory_space_constraint(array, pltpu.HBM)


def store_kernel(
    rows_ref, place_ref, left_ref, right_ref, moment_ref,
    update_ref, new_left_ref, new_right_ref, new_moment_ref, update, semaphores,
):
    pairs = ((left_ref, new_left_ref), (right_ref, new_right_ref), (moment_ref, new_moment_ref))
    copies = [
        pltpu.make_async_copy(src, dst, semaphores.at[i]) for i, (src, dst) in enumerate(pairs)
    ]
    for copy in copies:
        copy.start()
    picked = dot(place_ref[...], rows_ref[...].reshape(place_ref.shape[1], LANES))
    update[...] = picked.astype(BF16).reshape(update.shape)
    copies.append(pltpu.make_async_copy(update, update_ref, semaphores.at[3]))
    copies[3].start()
    for copy in copies:
        copy.wait()


def local(gradient, owner_slot, stat_left, stat_right, second_moment, basis_left, basis_right):
    layers, row_dev, columns = gradient.shape[1:]
    capacity, quarter, order = basis_right.shape
    blocks_per = columns // order
    chips = LINE * LINE
    many = layers * blocks_per * row_dev
    vmem = pl.BlockSpec(memory_space=pltpu.VMEM)
    hbm = pl.BlockSpec(memory_space=pltpu.HBM)
    dma = pltpu.SemaphoreType.DMA
    message = (chips, 4 * row_dev, quarter)
    stat = (capacity, quarter, order)
    full = (capacity, order, order)
    results = pl.pallas_call(
        kernel,
        name="soap_step",
        out_shape=(
            pltpu.VMEM(message, BF16),
            pltpu.VMEM((many, chips * 4 * row_dev), BF16),
            pltpu.VMEM(stat, F32),
            pltpu.VMEM(stat, F32),
            pltpu.VMEM(stat, F32),
        ),
        in_specs=[hbm] * 7,
        out_specs=[vmem] * 5,
        scratch_shapes=[
            pltpu.VMEM(owner_slot.shape, I32),
            pltpu.VMEM(gradient.shape[1:], BF16),
            pltpu.VMEM((4, many, quarter), BF16),
            pltpu.VMEM((3, many, quarter), BF16),
            pltpu.VMEM((2, many, quarter), BF16),
            pltpu.VMEM((chips * 2 * row_dev, many), BF16),
            pltpu.VMEM((256, 256), BF16),
            pltpu.VMEM((256, 256), BF16),
            pltpu.VMEM((256, 256), BF16),
            pltpu.VMEM(message, BF16),
            pltpu.VMEM(message, BF16),
            pltpu.VMEM(full, BF16),
            pltpu.VMEM(full, BF16),
            pltpu.VMEM(full, BF16),
            pltpu.VMEM((capacity, order, quarter), BF16),
            pltpu.VMEM((capacity, quarter, order), BF16),
            pltpu.VMEM(stat, F32),
            pltpu.VMEM((capacity, quarter, order), BF16),
            pltpu.VMEM((capacity, order, quarter), BF16),
            pltpu.VMEM((capacity, order, quarter), BF16),
            pltpu.VMEM((capacity, order, quarter), BF16),
            pltpu.VMEM(message, BF16),
            pltpu.VMEM(stat, F32),
            pltpu.VMEM(stat, F32),
            pltpu.VMEM(stat, F32),
            dma((10,)),
            dma, dma((2,)),
            dma, dma((2,)),
            dma, dma,
            dma, dma((2,)), dma((2,)),
            dma, dma, dma,
            dma, dma, dma,
            dma, dma((2,)),
            dma, dma((2,)),
            dma, dma,
            pltpu.SemaphoreType.REGULAR((5,)),
        ],
        compiler_params=pltpu.CompilerParams(
            collective_id=0, has_side_effects=True, vmem_limit_bytes=40 << 20
        ),
    )(*(stay(a) for a in (owner_slot, gradient[0], stat_left, stat_right, second_moment, basis_left, basis_right)))
    return pl.pallas_call(
        store_kernel,
        name="store",
        out_shape=(
            jax.ShapeDtypeStruct((layers, row_dev, blocks_per, quarter), BF16),
            *(jax.ShapeDtypeStruct(stat, F32) for _ in range(3)),
        ),
        in_specs=[vmem] * 5,
        out_specs=[hbm] * 4,
        scratch_shapes=[
            pltpu.VMEM((layers, row_dev, blocks_per, quarter), BF16),
            dma((4,)),
        ],
        compiler_params=pltpu.CompilerParams(vmem_limit_bytes=8 << 20),
    )(*results)


def solution(mesh):
    placed = (
        P("dp", None, "fsdp", None),
        P(),
        P("fsdp", "dp", None),
        P("fsdp", "dp", None),
        P("fsdp", "dp", None),
        P("fsdp", None, "dp"),
        P("fsdp", "dp", None),
    )
    return jax.shard_map(
        local,
        mesh=mesh,
        in_specs=placed,
        out_specs=(
            P(None, "fsdp", None, "dp"),
            P("fsdp", "dp", None),
            P("fsdp", "dp", None),
            P("fsdp", "dp", None),
        ),
        check_vma=False,
    )
```
